128 devices in a mesh: gx: 8 (over z, core), gy: 16 (over y, x).
Axes of the slice: x: 4, y: 4, z: 4, core: 2. Of those that a mesh axis runs over, the one named last changes fastest.
Arguments:
- increment: bfloat16 [128, 256, 384], P('gx', 'gy'), may hold values from -6 to 6
- vertical: bfloat16 [384, 384], replicated, may hold values from -0.3125 to 0.3125
- col_reach: float32 [384], replicated
- stretch_x: float32 [128, 256], P('gx', 'gy')
- stretch_y: float32 [128, 256], P('gx', 'gy')
Outputs:
- covaried: float32 [128, 256, 384], P('gx', 'gy')
The draws below stay inside these ranges and needn't reach their ends.
All inputs are finite; a program needn't handle non-finite values.
Results may differ from the reference program's by a relative error of at most 0.0003.
Values sent between devices are 32-bit elements; how exact they have to be, the bound alone decides.
A program may use at most 64 MiB of HBM per device.

```python
import math
import jax
import jax.numpy as jnp
from jax import lax

C = 384
GRID_POINTS_X = 128
GRID_POINTS_Y = 256


def draw_col_reach(key, part):
    key = jax.random.fold_in(key, 11)
    key_pick, key_slow, key_fast = jax.random.split(key, 3)
    share = 0.5
    picked = jax.random.uniform(key_pick, (C,), jnp.float32) < share
    slow_reach = jnp.exp(jax.random.uniform(key_slow, (C,), jnp.float32, math.log(0.5), 0.0))
    fast_reach = jnp.exp(jax.random.uniform(key_fast, (C,), jnp.float32, math.log(0.02), math.log(0.08)))
    return jnp.where(picked, slow_reach, fast_reach).astype(jnp.float32)


def draw_stretch_x(key, part):
    key = jax.random.fold_in(key, 21)
    root_key, key_sequence = jax.random.split(key, 2)
    base = jnp.exp(jax.random.uniform(root_key, (GRID_POINTS_X, GRID_POINTS_Y), jnp.float32, math.log(0.5), math.log(2.0)))
    device_positions = jax.random.randint(key_sequence, (3,), 0, GRID_POINTS_X)
    struck = jnp.any(jnp.arange(GRID_POINTS_X)[:, None] == device_positions[None, :], axis=1)
    return jnp.where(struck[:, None], 8.0 / GRID_POINTS_X, base).astype(jnp.float32)


def draw_stretch_y(key, part):
    key = jax.random.fold_in(key, 31)
    root_key, key_sequence = jax.random.split(key, 2)
    base = jnp.exp(jax.random.uniform(root_key, (GRID_POINTS_X, GRID_POINTS_Y), jnp.float32, math.log(0.5), math.log(2.0)))
    device_positions = jax.random.randint(key_sequence, (3,), 0, GRID_POINTS_Y)
    struck = jnp.any(jnp.arange(GRID_POINTS_Y)[:, None] == device_positions[None, :], axis=1)
    return jnp.where(struck[None, :], 8.0 / GRID_POINTS_Y, base).astype(jnp.float32)


def steps_of(rng, shape, cuts, low, largest):
    def one(position, shards_of):
        steps = jax.random.uniform(jax.random.fold_in(jax.random.fold_in(rng, 6), position), (shards_of,), jnp.float32, low / len(cuts), largest / len(cuts))
        return jnp.repeat(jnp.exp(steps), shape[position] // shards_of).reshape((-1,) + (1,) * (len(shape) - position - 1))

    level = one(*cuts[0])
    for cut in cuts[1:]:
        level = level * one(*cut)
    return level


def scatter_about(rng, shape, deviation, bound, cuts=(), dtype=jnp.bfloat16):
    values = deviation * jax.random.normal(rng, shape, jnp.float32)
    if cuts:
        values = values * steps_of(rng, shape, cuts, -0.22, 0.18)
    return jnp.clip(values, -bound, bound).astype(dtype)


def setup_inputs(seed: int = 0) -> dict:
    key_of = jax.random.split(jax.random.key(seed), 6)
    increment = scatter_about(key_of[0], (GRID_POINTS_X, GRID_POINTS_Y, C), 1.0, 6.0, ((0, 8), (1, 16)))
    vertical = scatter_about(key_of[1], (C, C), C ** -0.5, 0.3125)
    col_reach = draw_col_reach(jax.random.fold_in(key_of[5], 71), 0)
    stretch_x = draw_stretch_x(jax.random.fold_in(key_of[5], 71), 0)
    stretch_y = draw_stretch_y(jax.random.fold_in(key_of[5], 71), 0)
    return {"increment": increment, "vertical": vertical, "col_reach": col_reach, "stretch_x": stretch_x, "stretch_y": stretch_y}


def cascade(values_in, stretch, scale, reverse):

    def advance(section_state, inputs):
        values, stretch_row = inputs
        poles = jnp.exp(-1.0 / (stretch_row[:, None] * scale[None, :]))
        previous = values
        updated = []
        for section_index in range(4):
            previous = poles * section_state[section_index] + (1.0 - poles) * previous
            updated.append(previous)
        return (jnp.stack(updated), previous)
    initial = jnp.zeros((4,) + values_in.shape[1:], jnp.float32)
    unused, filtered = lax.scan(advance, initial, (values_in, stretch), reverse=reverse)
    return filtered

def reference(increment, vertical, col_reach, stretch_x, stretch_y):
    mixed_field = jnp.dot(increment.reshape(GRID_POINTS_X * GRID_POINTS_Y, C), vertical, preferred_element_type=jnp.float32).reshape(GRID_POINTS_X, GRID_POINTS_Y, C)
    length_scale_x = col_reach * GRID_POINTS_X
    filtered = cascade(mixed_field, stretch_x, length_scale_x, False)
    filtered = cascade(filtered, stretch_x, length_scale_x, True)
    turned = jnp.swapaxes(filtered, 0, 1)
    scale_y = col_reach * GRID_POINTS_Y
    turned = cascade(turned, stretch_y.T, scale_y, False)
    turned = cascade(turned, stretch_y.T, scale_y, True)
    restored = jnp.swapaxes(turned, 0, 1)
    amplitude = 10.0 * jnp.minimum(col_reach, 0.25) * math.sqrt(GRID_POINTS_X * GRID_POINTS_Y)
    return restored * amplitude[None, None, :]
```

```python
import functools
import math

import jax
import jax.numpy as jnp
from jax import lax
from jax.experimental import pallas as pl
from jax.experimental.pallas import tpu as pltpu
from jax.sharding import PartitionSpec as P

MESH = pl.DeviceIdType.MESH
B = 16
NX, NY = 8, 16
C, W, CT = 384, 128, 3
SX, SY = 6, 3
MX, MY = 8 * SX, 8 * SY
COEFS = 14
TX, TY = 88, 48
PAIRS = [(a, b) for a in range(4) for b in range(a, 4)]


def cascade(state, u, p, q):
    out = []
    for k in range(4):
        u = p * state[k] + q * u
        out.append(u)
    return out, u


def toeplitz(t, s, add):
    out = []
    for k in range(4):
        total = add[k]
        for m in range(k + 1):
            total = total + t[k - m] * s[m]
        out.append(total)
    return out


def transitions(rates, inverse_scale, put):
    for ct in range(CT):
        scale = inverse_scale[:, ct * W:(ct + 1) * W]
        c = None
        g = [None] * 10
        for i in range(B):
            p = jnp.exp(rates[:, i:i + 1] * scale)
            q = 1.0 - p
            if c is None:
                d = [jnp.ones_like(p), q]
                d.append(q * d[1])
                d.append(q * d[2])
            else:
                d = [c[0]]
                for k in range(1, 4):
                    d.append(c[k] + q * d[k - 1])
            c = [p * x for x in d]
            e = [q * x for x in c]
            for n, (a, b) in enumerate(PAIRS):
                term = d[a] * e[b]
                g[n] = term if g[n] is None else g[n] + term
        for k in range(4):
            put(k, ct, c[k])
        for n in range(10):
            put(4 + n, ct, g[n])


def chain(n, rows, got, coefs, reply):
    zero = jnp.zeros((rows, W), jnp.float32)

    def at(ref, j, k):
        return ref[j, k * rows:(k + 1) * rows, :]

    def ahead(j, s):
        for k in range(4):
            reply[j, k * rows:(k + 1) * rows, :] = s[k]
        t = [at(coefs, j, k) for k in range(4)]
        return tuple(toeplitz(t, s, [at(got, j, k) for k in range(4)]))

    lax.fori_loop(0, n, ahead, (zero,) * 4, unroll=True)

    def back(i, b):
        j = n - 1 - i
        for k in range(4):
            reply[j, (4 + k) * rows:(5 + k) * rows, :] = b[k]
        s = [at(reply, j, k) for k in range(4)]
        g = [at(coefs, j, 4 + m) for m in range(10)]
        add = []
        for a in range(4):
            total = at(got, j, 4 + a)
            for m in range(4):
                x, y = min(a, 3 - m), max(a, 3 - m)
                total = total + g[PAIRS.index((x, y))] * s[m]
            add.append(total)
        t = [at(coefs, j, k) for k in range(4)]
        return tuple(toeplitz(t, b, add))

    lax.fori_loop(0, n, back, (zero,) * 4, unroll=True)


def kernel(inc, vert, reach, sx, sy, out,
           u, px, py, mid, xs1, xr1, xs2, xr2, ys1, yr1, ys2, yr2,
           tgx, tgy, sxs, sxr, sys_, syr, send_sem, recv_sem):
    gx, gy = lax.axis_index("gx"), lax.axis_index("gy")

    def peer_x(r):
        return lax.rem(gx + r, NX)

    def peer_y(r):
        return lax.rem(gy + r, NY)

    barrier = pltpu.get_barrier_semaphore()
    for r in range(1, NX):
        pl.semaphore_signal(barrier, inc=1, device_id=(peer_x(r), gy), device_id_type=MESH)
    for r in range(1, NY):
        pl.semaphore_signal(barrier, inc=1, device_id=(gx, peer_y(r)), device_id_type=MESH)

    def start_x(src, dst, at):
        for r in range(1, NX):
            pltpu.make_async_remote_copy(
                src.at[peer_x(r)], dst.at[gx], send_sem.at[at], recv_sem.at[at],
                device_id=(peer_x(r), gy), device_id_type=MESH).start()

    def start_y(src, dst, at):
        for r in range(1, NY):
            pltpu.make_async_remote_copy(
                src.at[peer_y(r)], dst.at[gy], send_sem.at[at], recv_sem.at[at],
                device_id=(gx, peer_y(r)), device_id_type=MESH).start()

    def wait_recv(dst, n, at):
        part = dst.at[pl.ds(0, n - 1)]
        pltpu.make_async_copy(part, part, recv_sem.at[at]).wait()

    def wait_send(src, n, at):
        part = src.at[pl.ds(0, n - 1)]
        pltpu.make_async_copy(part, part, send_sem.at[at]).wait()

    rate_x = -1.0 / sx[...].T
    rate_y = -1.0 / sy[...]
    for half in range(2):
        sxs.reshape(NX * 8, W)[pl.ds(half, 8, stride=8), 0:B] = rate_x[8 * half:8 * half + 8]
        sys_.reshape(NY * 8, W)[pl.ds(64 * half, 8, stride=8), 0:B] = rate_y[8 * half:8 * half + 8]
    inverse_x = 1.0 / (reach[...] * float(NX * B))
    inverse_y = 1.0 / (reach[...] * float(NY * B))

    mixed = jnp.dot(inc[...], vert[...], preferred_element_type=jnp.float32)
    for ct in range(CT):
        u[ct] = mixed[:, ct * W:(ct + 1) * W]

    def tiles(ref, rows):
        return jnp.concatenate([ref[ct, rows, :] for ct in range(CT)], axis=1)

    def put_tiles(ref, rows, value):
        for ct in range(CT):
            ref[ct, rows, :] = value[:, ct * W:(ct + 1) * W]

    def sweep(source, poles, sink, rows_of, first, second):
        state = first
        for i in range(B):
            p = tiles(poles, pl.ds(i * B, B))
            state, w = cascade(state, tiles(source, rows_of(i)), p, 1.0 - p)
            put_tiles(mid, pl.ds(i * B, B), w)
        ahead, state = state, second
        for i in reversed(range(B)):
            p = tiles(poles, pl.ds(i * B, B))
            state, w = cascade(state, tiles(mid, pl.ds(i * B, B)), p, 1.0 - p)
            if sink is not None:
                sink(i, w)
        return ahead + state

    def pack_x(states, ref):
        flat = ref.reshape(NX * MX, W)
        for k in range(8):
            for l in range(2):
                for ct in range(CT):
                    flat[pl.ds(k * SX + l * CT + ct, 8, stride=MX), :] = (
                        states[k][8 * l:8 * l + 8, ct * W:(ct + 1) * W])

    def unpack_x(ref):
        flat = ref.reshape(NX * MX, W)
        return [jnp.concatenate([jnp.concatenate(
            [flat[pl.ds(k * SX + l * CT + ct, 8, stride=MX), :] for ct in range(CT)], axis=1)
            for l in range(2)], axis=0) for k in range(8)]

    def pack_y(states, ref):
        flat = ref.reshape(NY * MY, W)
        for k in range(8):
            for l in range(2):
                for ct in range(CT):
                    flat[pl.ds(8 * l * MY + k * SY + ct, 8, stride=MY), :] = (
                        states[k][8 * l:8 * l + 8, ct * W:(ct + 1) * W])

    def unpack_y(ref):
        flat = ref.reshape(NY * MY, W)
        return [jnp.concatenate([jnp.concatenate(
            [flat[pl.ds(8 * l * MY + k * SY + ct, 8, stride=MY), :] for ct in range(CT)], axis=1)
            for l in range(2)], axis=0) for k in range(8)]

    for i in range(B):
        put_tiles(px, pl.ds(i * B, B), jnp.exp(rate_x[:, i:i + 1] * inverse_x))
    zeros = [jnp.zeros((B, C), jnp.float32)] * 4
    ends = sweep(u, px, None, lambda i: pl.ds(i * B, B), zeros, zeros)
    pack_x(ends, xs1)

    pl.semaphore_wait(barrier, NX + NY - 2)
    start_x(sxs, sxr, 0)
    start_x(xs1, xr1, 2)
    start_y(sys_, syr, 1)
    sxr[gx] = sxs[gx]
    syr[gy] = sys_[gy]
    xr1[gx] = xs1[gx]
    for i in range(B):
        put_tiles(py, pl.ds(i * B, B), jnp.exp(rate_y[:, i:i + 1] * inverse_y))

    wait_recv(sxr, NX, 0)
    flat = sxr.reshape(NX * 8, W)
    rates = jnp.concatenate([flat[pl.ds(l, 8, stride=8), 0:B] for l in range(2)], axis=0)
    flat_tgx = tgx.reshape(NX * TX, W)

    def put_x(k, ct, value):
        for l in range(2):
            flat_tgx[pl.ds(k * SX + l * CT + ct, 8, stride=TX), :] = value[8 * l:8 * l + 8]

    transitions(rates, inverse_x, put_x)

    wait_recv(xr1, NX, 2)
    chain(NX, SX, xr1, tgx, xs2)
    start_x(xs2, xr2, 3)
    xr2[gx] = xs2[gx]

    wait_recv(syr, NY, 1)
    flat = syr.reshape(NY * 8, W)
    rates = flat[pl.ds(0, NY, stride=8), 0:B]
    flat_tgy = tgy.reshape(NY * TY, W)

    def put_y(k, ct, value):
        for l in range(2):
            flat_tgy[pl.ds(8 * l * TY + k * SY + ct, 8, stride=TY), :] = value[8 * l:8 * l + 8]

    transitions(rates, inverse_y, put_y)

    wait_recv(xr2, NX, 3)
    states = unpack_x(xr2)

    def keep(i, w):
        put_tiles(u, pl.ds(i * B, B), w)

    sweep(u, px, keep, lambda i: pl.ds(i * B, B), states[:4], states[4:])

    def across(i):
        return pl.ds(i, B, stride=B)

    ends = sweep(u, py, None, across, zeros, zeros)
    pack_y(ends, ys1)
    start_y(ys1, yr1, 4)
    yr1[gy] = ys1[gy]
    wait_recv(yr1, NY, 4)
    chain(NY, SY, yr1, tgy, ys2)
    start_y(ys2, yr2, 5)
    yr2[gy] = ys2[gy]
    amplitude = 10.0 * jnp.minimum(reach[...], 0.25) * math.sqrt(NX * B * NY * B)
    wait_recv(yr2, NY, 5)
    states = unpack_y(yr2)

    def finish(i, w):
        put_tiles(u, across(i), w * amplitude)

    sweep(u, py, finish, across, states[:4], states[4:])
    for ct in range(CT):
        out[:, ct * W:(ct + 1) * W] = u[ct]

    wait_send(sxs, NX, 0)
    wait_send(sys_, NY, 1)
    wait_send(xs1, NX, 2)
    wait_send(xs2, NX, 3)
    wait_send(ys1, NY, 4)
    wait_send(ys2, NY, 5)


def shards(increment, vertical, col_reach, stretch_x, stretch_y):
    f32 = jnp.float32
    field = pltpu.VMEM((CT, B * B, W), f32)
    mx, my = pltpu.VMEM((NX, MX, W), f32), pltpu.VMEM((NY, MY, W), f32)
    vmem = pl.BlockSpec(memory_space=pltpu.VMEM)
    result = pl.pallas_call(
        kernel,
        out_shape=jax.ShapeDtypeStruct((B * B, C), f32),
        in_specs=[vmem] * 5,
        out_specs=vmem,
        scratch_shapes=[
            field, field, field, field, mx, mx, mx, mx, my, my, my, my,
            pltpu.VMEM((NX, TX, W), f32), pltpu.VMEM((NY, TY, W), f32),
            pltpu.VMEM((NX, 8, W), f32), pltpu.VMEM((NX, 8, W), f32),
            pltpu.VMEM((NY, 8, W), f32), pltpu.VMEM((NY, 8, W), f32),
            pltpu.SemaphoreType.DMA((6,)), pltpu.SemaphoreType.DMA((6,)),
        ],
        compiler_params=pltpu.CompilerParams(
            collective_id=0, has_side_effects=True, vmem_limit_bytes=32 * 2**20),
        name="covariance",
    )(increment.reshape(B * B, C), vertical, col_reach.reshape(1, C), stretch_x, stretch_y)
    return result.reshape(B, B, C)


def solution(mesh):
    in_specs = (P("gx", "gy", None), P(), P(), P("gx", "gy"), P("gx", "gy"))
    out_specs = P("gx", "gy", None)
    return jax.shard_map(shards, mesh=mesh, in_specs=in_specs, out_specs=out_specs, check_vma=False)
```

```python
import functools
import math

import jax
import jax.numpy as jnp
from jax import lax
from jax.experimental import pallas as pl
from jax.experimental.pallas import tpu as pltpu
from jax.sharding import PartitionSpec as P

MESH = pl.DeviceIdType.MESH
B = 16
NX, NY, NZ = 8, 16, 4
C, W, CT = 384, 128, 3
OFFSETS_Y = sorted([(a, b) for a in range(4) for b in range(4) if a or b],
                   key=lambda o: -min(o[0], 4 - o[0]) - min(o[1], 4 - o[1]))
PAIRS = [(a, b) for a in range(4) for b in range(a, 4)]


def cascade(state, u, p, q):
    out = []
    for k in range(4):
        u = p * state[k] + q * u
        out.append(u)
    return out, u


def toeplitz(t, s, add):
    out = []
    for k in range(4):
        total = add[k]
        for m in range(k + 1):
            total = total + t[k - m] * s[m]
        out.append(total)
    return out


def reflect(g, s, add):
    out = []
    for a in range(4):
        total = add[a]
        for m in range(4):
            total = total + g[PAIRS.index((min(a, 3 - m), max(a, 3 - m)))] * s[m]
        out.append(total)
    return out


def transfer(rates, scale, reflecting):
    c, g = None, [None] * 10
    for rate in rates:
        p = jnp.exp(rate * scale)
        q = 1.0 - p
        if c is None:
            d = [jnp.ones_like(p), q]
            d.append(q * d[1])
            d.append(q * d[2])
        else:
            d = [c[0]]
            for k in range(1, 4):
                d.append(c[k] + q * d[k - 1])
        c = [p * x for x in d]
        if reflecting:
            e = [q * x for x in c]
            for n, (a, b) in enumerate(PAIRS):
                term = d[a] * e[b]
                g[n] = term if g[n] is None else g[n] + term
    return (c, g) if reflecting else c


def columns(tile):
    return [tile[:, i:i + 1] for i in range(B)]


def sweep(source, poles, mid, rows_of, first, second, sink=None):
    state = first
    for i in range(B):
        rows = pl.ds(i * B, B)
        p = poles[rows, :]
        state, w = cascade(state, source[rows_of(i), :], p, 1.0 - p)
        mid[rows, :] = w
    ahead, state = state, second
    for i in reversed(range(B)):
        rows = pl.ds(i * B, B)
        p = poles[rows, :]
        state, w = cascade(state, mid[rows, :], p, 1.0 - p)
        if sink is not None:
            sink(i, w)
    return ahead + state


def chain(got, coefs, reply):
    zero = [jnp.zeros((1, W), jnp.float32)] * 4

    def at(ref, j, k):
        return ref[j, k:k + 1, :]

    s, entered = zero, []
    for j in range(NY):
        entered.append(s)
        for k in range(4):
            reply[j, k:k + 1, :] = s[k]
        s = toeplitz([at(coefs, j, k) for k in range(4)], s, [at(got, j, k) for k in range(4)])
    b = zero
    for j in reversed(range(NY)):
        for k in range(4):
            reply[j, 4 + k:5 + k, :] = b[k]
        g = [at(coefs, j, 4 + n) for n in range(10)]
        add = reflect(g, entered[j], [at(got, j, 4 + k) for k in range(4)])
        b = toeplitz([at(coefs, j, k) for k in range(4)], b, add)


def kernel(inc_hbm, vert_hbm, reach_hbm, sx_hbm, sy_hbm, out,
           inc, vert, reach_line, sx, sy, load_sem, u, px, py, mid,
           ends_x, pair, own, chips, passing, to_z, from_z, back, entering, ys1, yr1, ys2, yr2,
           tgy, sxs, sxr, sys_, syr, pole_send, pole_recv, pair_send, pair_recv, z_send, z_recv,
           back_send, back_recv, y_send, y_recv):
    gx, gy = lax.axis_index("gx"), lax.axis_index("gy")
    z, core = gx // 2, lax.rem(gx, 2)
    other = (gx + 1 - 2 * core, gy)

    def peer_y(dy, dx):
        return lax.rem(gy // 4 + dy, 4) * 4 + lax.rem(gy + dx, 4)

    barrier = pltpu.get_barrier_semaphore()
    for r in range(1, NX):
        pl.semaphore_signal(barrier, inc=1, device_id=(lax.rem(gx + r, NX), gy), device_id_type=MESH)
    for offset in OFFSETS_Y:
        pl.semaphore_signal(barrier, inc=1, device_id=(gx, peer_y(*offset)), device_id_type=MESH)

    loads = [pltpu.make_async_copy(src, dst, load_sem.at[n]) for n, (src, dst) in enumerate(
        [(sx_hbm, sx), (reach_hbm, reach_line), (vert_hbm, vert), (inc_hbm, inc), (sy_hbm, sy)])]
    for load in loads:
        load.start()

    def remote(src, dst, sent, got, device):
        return pltpu.make_async_remote_copy(src, dst, sent, got, device_id=device, device_id_type=MESH)

    def start_y(src, dst, sent, got):
        for offset in OFFSETS_Y:
            peer = peer_y(*offset)
            remote(src.at[peer], dst.at[gy], sent, got, (gx, peer)).start()
        dst[gy] = src[gy]

    def wait_for(part, sem):
        pltpu.make_async_copy(part, part, sem).wait()

    def lanes(ct):
        return slice(ct * W, (ct + 1) * W)

    loads[0].wait()
    loads[1].wait()
    reach = reach_line[...].reshape(1, C)
    rate_x = -1.0 / sx[...].T
    inverse_x = 1.0 / (reach * float(NX * B))
    inverse_y = 1.0 / (reach * float(NY * B))
    for i in range(B):
        for ct in range(CT):
            px[ct, pl.ds(i * B, B), :] = jnp.exp(rate_x[:, i:i + 1] * inverse_x[:, lanes(ct)])
    loads[4].wait()
    rate_y = -1.0 / sy[...]
    for half in range(2):
        sxs[half, :, 0:B] = rate_x[8 * half:8 * half + 8]
        sys_.reshape(NY * 8, W)[pl.ds(64 * half, 8, stride=8), 0:B] = rate_y[8 * half:8 * half + 8]
    loads[2].wait()
    loads[3].wait()
    mixed = jnp.dot(inc[...], vert[...], preferred_element_type=jnp.float32)
    for ct in range(CT):
        u[ct] = mixed[:, lanes(ct)]

    pl.semaphore_wait(barrier, NX + NY - 2)
    remote(sxs.at[1 - core], sxr.at[gx], pole_send.at[0], pole_recv.at[0], other).start()
    for r in (2, 1, 3):
        for c in range(2):
            peer = 2 * lax.rem(z + r, NZ) + c
            remote(sxs.at[c], sxr.at[gx], pole_send.at[1], pole_recv.at[1], (peer, gy)).start()
    sxr[gx] = sxs[core]

    zeros = [jnp.zeros((B, W), jnp.float32)] * 4
    nothing = [jnp.zeros((8, W), jnp.float32)] * 4

    def along(i):
        return pl.ds(i * B, B)

    def across(i):
        return pl.ds(i, B, stride=B)

    for ct in range(CT):
        ends = sweep(u.at[ct], px.at[ct], mid.at[ct], along, zeros, zeros)
        for half in range(2):
            for k in range(8):
                ends_x[ct, half, k] = ends[k][8 * half:8 * half + 8]
        remote(ends_x.at[ct, 1 - core], pair.at[ct, core], pair_send.at[ct], pair_recv.at[ct], other).start()
        pair[ct, core] = ends_x[ct, core]

    def start_z(ct, r, kind):
        peer = lax.rem(z + r, NZ)
        return remote(to_z.at[ct, kind], from_z.at[ct, z, kind], z_send.at[ct, peer, kind],
                      z_recv.at[ct, z, kind], (2 * peer + core, gy))

    def blocks(ct):
        t0, t1 = [own[ct, k] for k in range(4)], [own[ct, 4 + k] for k in range(4)]
        g1 = [own[ct, 8 + n] for n in range(10)]
        return t0, t1, g1, [[pair[ct, b, k] for k in range(8)] for b in range(2)]

    wait_for(sxr.at[0], pole_recv.at[0])
    first, second = columns(sxr[2 * z]), columns(sxr[2 * z + 1])
    for ct in range(CT):
        scale = inverse_x[:, lanes(ct)]
        t, g = transfer(second, scale, True)
        for k, value in enumerate(transfer(first, scale, False) + t + g):
            own[ct, k] = value
    for ct in range(CT):
        wait_for(pair.at[ct, 0], pair_recv.at[ct])
        t0, t1, g1, (e0, e1) = blocks(ct)
        ahead = toeplitz(t1, e0[:4], e1[:4])
        behind = toeplitz(t0, reflect(g1, e0[:4], e1[4:]), e0[4:])
        for k in range(4):
            to_z[ct, 0, k] = ahead[k]
            to_z[ct, 1, k] = behind[k]
        for r in (2, 1, 3):
            pl.when(z < NZ - 1)(lambda ct=ct, r=r: start_z(ct, r, 0).start())
            pl.when(lax.rem(z + r, NZ) < z)(lambda ct=ct, r=r: start_z(ct, r, 1).start())

    start_y(sys_, syr, pole_send.at[2], pole_recv.at[2])
    wait_for(sxr.at[pl.ds(0, NX - 2)], pole_recv.at[1])
    for ct in range(CT):
        scale = inverse_x[:, lanes(ct)]

        def stretches(m):
            return columns(sxr[2 * m]) + columns(sxr[2 * m + 1])

        def left(m, _):
            for k, value in enumerate(transfer(stretches(m), scale, False)):
                chips[m, ct, k] = value
            return 0

        def right(m, _):
            t, g = transfer(stretches(m), scale, True)
            for k, value in enumerate(t + g):
                chips[m, ct, k] = value
            return 0

        lax.fori_loop(0, z, left, 0)
        lax.fori_loop(z + 1, NZ, right, 0)

        def chip(m):
            return [chips[m, ct, k] for k in range(4)]

        def came(m, kind):
            wait_for(from_z.at[ct, m, kind], z_recv.at[ct, m, kind])
            return [from_z[ct, m, kind, k] for k in range(4)]

        def ahead(m, s):
            return toeplitz(chip(m), s, came(m, 0))

        def onward(m, s):
            s = ahead(m, s)
            for k in range(4):
                passing[ct, m + 1, k] = s[k]
            return s

        def behind(i, b):
            m = NZ - 1 - i
            g = [chips[m, ct, 4 + n] for n in range(10)]
            return toeplitz(chip(m), b, reflect(g, [passing[ct, m, k] for k in range(4)], came(m, 1)))

        s0 = lax.fori_loop(0, z, ahead, nothing)
        t0, t1, g1, (e0, e1) = blocks(ct)
        s1 = toeplitz(t0, s0, e0[:4])
        s2 = toeplitz(t1, s1, e1[:4])
        for k in range(4):
            passing[ct, z + 1, k] = s2[k]
        lax.fori_loop(z + 1, NZ - 1, onward, s2)
        b1 = lax.fori_loop(0, NZ - 1 - z, behind, nothing)
        b0 = toeplitz(t1, b1, reflect(g1, s1, e1[4:]))
        for b, states in enumerate([s0 + b0, s1 + b1]):
            for k in range(8):
                back[ct, b, k] = states[k]
        remote(back.at[ct, 1 - core], entering.at[ct, core], back_send.at[ct], back_recv.at[ct], other).start()
        entering[ct, core] = back[ct, core]

    for i in range(B):
        for ct in range(CT):
            py[ct, pl.ds(i * B, B), :] = jnp.exp(rate_y[:, i:i + 1] * inverse_y[:, lanes(ct)])

    for ct in range(CT):
        wait_for(entering.at[ct, 0], back_recv.at[ct])
        states = [jnp.concatenate([entering[ct, half, k] for half in range(2)], axis=0) for k in range(8)]

        def keep(i, w):
            u[ct, along(i), :] = w

        sweep(u.at[ct], px.at[ct], mid.at[ct], along, states[:4], states[4:], keep)
        ends = sweep(u.at[ct], py.at[ct], mid.at[ct], across, zeros, zeros)
        flat = ys1.at[ct].reshape(NY * 8, W)
        for k in range(8):
            for l in range(2):
                flat[pl.ds(64 * l + k, 8, stride=8), :] = ends[k][8 * l:8 * l + 8]
        start_y(ys1.at[ct], yr1.at[ct], y_send.at[0, ct], y_recv.at[0, ct])

    wait_for(syr.at[pl.ds(0, NY - 1)], pole_recv.at[2])
    rates = columns(syr.reshape(NY * 8, W)[pl.ds(0, NY, stride=8), 0:B])
    for ct in range(CT):
        t, g = transfer(rates, inverse_y[:, lanes(ct)], True)
        flat = tgy.at[ct].reshape(NY * 16, W)
        for k, value in enumerate(t + g):
            for l in range(2):
                flat[pl.ds(128 * l + k, 8, stride=16), :] = value[8 * l:8 * l + 8]

    for ct in range(CT):
        wait_for(yr1.at[ct, pl.ds(0, NY - 1)], y_recv.at[0, ct])
        chain(yr1.at[ct], tgy.at[ct], ys2.at[ct])
        start_y(ys2.at[ct], yr2.at[ct], y_send.at[1, ct], y_recv.at[1, ct])

    amplitude = 10.0 * jnp.minimum(reach, 0.25) * math.sqrt(NX * B * NY * B)
    for ct in range(CT):
        wait_for(yr2.at[ct, pl.ds(0, NY - 1)], y_recv.at[1, ct])
        flat = yr2.at[ct].reshape(NY * 8, W)
        states = [flat[pl.ds(k, NY, stride=8), :] for k in range(8)]

        def finish(i, w):
            u[ct, across(i), :] = w * amplitude[:, lanes(ct)]

        sweep(u.at[ct], py.at[ct], mid.at[ct], across, states[:4], states[4:], finish)
        out[:, lanes(ct)] = u[ct]

    wait_for(sxr.at[0], pole_send.at[0])
    wait_for(sxr.at[pl.ds(0, NX - 2)], pole_send.at[1])
    wait_for(syr.at[pl.ds(0, NY - 1)], pole_send.at[2])
    for ct in range(CT):
        wait_for(pair.at[ct, 0], pair_send.at[ct])
        for r in range(1, NZ):
            pl.when(z < NZ - 1)(lambda ct=ct, r=r: start_z(ct, r, 0).wait_send())
            pl.when(lax.rem(z + r, NZ) < z)(lambda ct=ct, r=r: start_z(ct, r, 1).wait_send())
        wait_for(entering.at[ct, 0], back_send.at[ct])
        wait_for(ys1.at[ct, pl.ds(0, NY - 1)], y_send.at[0, ct])
        wait_for(ys2.at[ct, pl.ds(0, NY - 1)], y_send.at[1, ct])


def shards(increment, vertical, col_reach, stretch_x, stretch_y):
    f32 = jnp.float32
    field = pltpu.VMEM((CT, B * B, W), f32)

    def states(*lead):
        return pltpu.VMEM(lead + (8, W), f32)

    def dma(*shape):
        return pltpu.SemaphoreType.DMA(shape)

    two, lines = states(CT, 2, 8), states(CT, NY)
    operands = (increment.reshape(B * B, C), vertical, col_reach, stretch_x, stretch_y)
    result = pl.pallas_call(
        kernel,
        out_shape=jax.ShapeDtypeStruct((B * B, C), f32),
        in_specs=[pl.BlockSpec(memory_space=pltpu.HBM)] * 5,
        out_specs=pl.BlockSpec(memory_space=pltpu.VMEM),
        scratch_shapes=[
            pltpu.VMEM((B * B, C), jnp.bfloat16), pltpu.VMEM((C, C), jnp.bfloat16), pltpu.VMEM((C,), f32),
            pltpu.VMEM((B, B), f32), pltpu.VMEM((B, B), f32), dma(5),
            field, field, field, field,
            two, two, states(CT, 18), states(NZ, CT, 14), states(CT, NZ + 1, 4),
            states(CT, 2, 4), states(CT, NZ, 2, 4), two, two,
            lines, lines, lines, lines, pltpu.VMEM((CT, NY, 16, W), f32),
            states(2), states(NX), states(NY), states(NY),
            dma(3), dma(3), dma(CT), dma(CT), dma(CT, NZ, 2), dma(CT, NZ, 2),
            dma(CT), dma(CT), dma(2, CT), dma(2, CT),
        ],
        compiler_params=pltpu.CompilerParams(
            collective_id=0, has_side_effects=True, vmem_limit_bytes=32 * 2**20),
        name="covariance",
    )(*[pltpu.with_memory_space_constraint(x, pltpu.HBM) for x in operands])
    return result.reshape(B, B, C)


def solution(mesh):
    in_specs = (P("gx", "gy", None), P(), P(), P("gx", "gy"), P("gx", "gy"))
    out_specs = P("gx", "gy", None)
    return jax.shard_map(shards, mesh=mesh, in_specs=in_specs, out_specs=out_specs, check_vma=False)
```

```python
import functools
import math

import jax
import jax.numpy as jnp
from jax import lax
from jax.experimental import pallas as pl
from jax.experimental.pallas import tpu as pltpu
from jax.sharding import PartitionSpec as P

MESH = pl.DeviceIdType.MESH
B = 16
NX, NY, NZ = 8, 16, 4
C, W, CT = 384, 128, 3
OFFSETS_Y = sorted([(a, b) for a in range(4) for b in range(4) if a or b],
                   key=lambda o: -min(o[0], 4 - o[0]) - min(o[1], 4 - o[1]))
PAIRS = [(a, b) for a in range(4) for b in range(a, 4)]


def cascade(state, u, p, q):
    out = []
    for k in range(4):
        u = p * state[k] + q * u
        out.append(u)
    return out, u


def toeplitz(t, s, add):
    out = []
    for k in range(4):
        total = add[k]
        for m in range(k + 1):
            total = total + t[k - m] * s[m]
        out.append(total)
    return out


def reflect(g, s, add):
    out = []
    for a in range(4):
        total = add[a]
        for m in range(4):
            total = total + g[PAIRS.index((min(a, 3 - m), max(a, 3 - m)))] * s[m]
        out.append(total)
    return out


def transfer(rates, scale, reflecting):
    c, g = None, [None] * 10
    for rate in rates:
        p = jnp.exp(rate * scale)
        q = 1.0 - p
        if c is None:
            d = [jnp.ones_like(p), q]
            d.append(q * d[1])
            d.append(q * d[2])
        else:
            d = [c[0]]
            for k in range(1, 4):
                d.append(c[k] + q * d[k - 1])
        c = [p * x for x in d]
        if reflecting:
            e = [q * x for x in c]
            for n, (a, b) in enumerate(PAIRS):
                term = d[a] * e[b]
                g[n] = term if g[n] is None else g[n] + term
    return (c, g) if reflecting else c


def columns(tile):
    return [tile[:, i:i + 1] for i in range(B)]


def sweep(source, poles, mid, rows_of, first, second, sink=None):
    state = first
    for i in range(B):
        rows = pl.ds(i * B, B)
        p = poles[rows, :]
        state, w = cascade(state, source[rows_of(i), :], p, 1.0 - p)
        mid[rows, :] = w
    ahead, state = state, second
    for i in reversed(range(B)):
        rows = pl.ds(i * B, B)
        p = poles[rows, :]
        state, w = cascade(state, mid[rows, :], p, 1.0 - p)
        if sink is not None:
            sink(i, w)
    return ahead + state


def chain(got, coefs, reply):
    zero = [jnp.zeros((1, W), jnp.float32)] * 4

    def at(ref, j, k):
        return ref[j, k:k + 1, :]

    s, entered = zero, []
    for j in range(NY):
        entered.append(s)
        for k in range(4):
            reply[j, k:k + 1, :] = s[k]
        s = toeplitz([at(coefs, j, k) for k in range(4)], s, [at(got, j, k) for k in range(4)])
    b = zero
    for j in reversed(range(NY)):
        for k in range(4):
            reply[j, 4 + k:5 + k, :] = b[k]
        g = [at(coefs, j, 4 + n) for n in range(10)]
        add = reflect(g, entered[j], [at(got, j, 4 + k) for k in range(4)])
        b = toeplitz([at(coefs, j, k) for k in range(4)], b, add)


def kernel(inc_hbm, vert_hbm, reach_hbm, sx_hbm, sy_hbm, out,
           inc, vert, reach_line, sx, sy, load_sem, u, px, py, mid,
           ends_x, pair, own, chips, passing, to_z, from_z, back, entering, ys1, yr1, ys2, yr2,
           tgy, sxs, sxr, sys_, syr, sent, z_sent, y_sent, beside_recv, chip_recv, lines_recv, pair_recv,
           z_recv, back_recv, gather_recv, reply_recv):
    gx, gy = lax.axis_index("gx"), lax.axis_index("gy")
    z, core = gx // 2, lax.rem(gx, 2)
    other = (gx + 1 - 2 * core, gy)
    owner = 2 * z + 1

    def peer_y(dy, dx):
        return lax.rem(gy // 4 + dy, 4) * 4 + lax.rem(gy + dx, 4)

    barrier = pltpu.get_barrier_semaphore()
    for r in range(1, NX):
        pl.semaphore_signal(barrier, inc=1, device_id=(lax.rem(gx + r, NX), gy), device_id_type=MESH)
    for offset in OFFSETS_Y:
        pl.semaphore_signal(barrier, inc=1, device_id=(owner, peer_y(*offset)), device_id_type=MESH)

    @pl.when(core == 1)
    def _():
        for offset in OFFSETS_Y:
            pl.semaphore_signal(barrier, inc=1, device_id=(owner - 1, peer_y(*offset)), device_id_type=MESH)

    loads = [pltpu.make_async_copy(src, dst, load_sem.at[n]) for n, (src, dst) in enumerate(
        [(sx_hbm, sx), (reach_hbm, reach_line), (vert_hbm, vert), (inc_hbm, inc), (sy_hbm, sy)])]
    for load in loads:
        load.start()

    def remote(src, dst, sent, got, device):
        return pltpu.make_async_remote_copy(src, dst, sent, got, device_id=device, device_id_type=MESH)

    def to_owners(src, dst, got):
        for offset in OFFSETS_Y:
            peer = peer_y(*offset)
            remote(src.at[peer], dst.at[core, gy], y_sent.at[0], got, (owner, peer)).start()

        @pl.when(core == 0)
        def _():
            remote(src.at[gy], dst.at[0, gy], y_sent.at[0], got, (owner, gy)).start()

        @pl.when(core == 1)
        def _():
            dst[1, gy] = src[gy]

    def wait_for(part, sem):
        pltpu.make_async_copy(part, part, sem).wait()

    def lanes(ct):
        return slice(ct * W, (ct + 1) * W)

    loads[0].wait()
    loads[1].wait()
    reach = reach_line[...].reshape(1, C)
    rate_x = -1.0 / sx[...].T
    inverse_x = 1.0 / (reach * float(NX * B))
    inverse_y = 1.0 / (reach * float(NY * B))
    for i in range(B):
        for ct in range(CT):
            px[ct, pl.ds(i * B, B), :] = jnp.exp(rate_x[:, i:i + 1] * inverse_x[:, lanes(ct)])
    loads[4].wait()
    rate_y = -1.0 / sy[...]
    for half in range(2):
        sxs[half, :, 0:B] = rate_x[8 * half:8 * half + 8]
        sys_.reshape(NY * 8, W)[pl.ds(64 * half, 8, stride=8), 0:B] = rate_y[8 * half:8 * half + 8]
    loads[2].wait()
    loads[3].wait()
    mixed = jnp.dot(inc[...], vert[...], preferred_element_type=jnp.float32)
    for ct in range(CT):
        u[ct] = mixed[:, lanes(ct)]

    zeros = [jnp.zeros((B, W), jnp.float32)] * 4
    nothing = [jnp.zeros((8, W), jnp.float32)] * 4

    def along(i):
        return pl.ds(i * B, B)

    def across(i):
        return pl.ds(i, B, stride=B)

    for ct in range(CT):
        ends = sweep(u.at[ct], px.at[ct], mid.at[ct], along, zeros, zeros)
        for half in range(2):
            for k in range(8):
                ends_x[ct, half, k] = ends[k][8 * half:8 * half + 8]

    pl.semaphore_wait(barrier, NX + NY - 2 + core * (NY - 1))
    remote(sxs.at[1 - core], sxr.at[gx], sent.at[0], beside_recv.at[0], other).start()
    for ct in range(CT):
        remote(ends_x.at[ct, 1 - core], pair.at[ct, core], sent.at[0], pair_recv.at[ct], other).start()
    for r in (2, 1, 3):
        for c in range(2):
            peer = 2 * lax.rem(z + r, NZ) + c
            remote(sxs.at[c], sxr.at[gx], sent.at[0], chip_recv.at[z], (peer, gy)).start()
    sxr[gx] = sxs[core]
    for ct in range(CT):
        pair[ct, core] = ends_x[ct, core]

    def start_z(ct, r, kind):
        peer = lax.rem(z + r, NZ)
        return remote(to_z.at[ct, kind], from_z.at[ct, z, kind], z_sent.at[0], z_recv.at[ct],
                      (2 * peer + core, gy))

    def blocks(ct):
        t0, t1 = [own[ct, k] for k in range(4)], [own[ct, 4 + k] for k in range(4)]
        g1 = [own[ct, 8 + n] for n in range(10)]
        return t0, t1, g1, [[pair[ct, b, k] for k in range(8)] for b in range(2)]

    wait_for(sxr.at[0], beside_recv.at[0])
    first, second = columns(sxr[2 * z]), columns(sxr[2 * z + 1])
    for ct in range(CT):
        scale = inverse_x[:, lanes(ct)]
        t, g = transfer(second, scale, True)
        for k, value in enumerate(transfer(first, scale, False) + t + g):
            own[ct, k] = value
        wait_for(pair.at[ct, 0], pair_recv.at[ct])
        t0, t1, g1, (e0, e1) = blocks(ct)
        ahead = toeplitz(t1, e0[:4], e1[:4])
        behind = toeplitz(t0, reflect(g1, e0[:4], e1[4:]), e0[4:])
        for k in range(4):
            to_z[ct, 0, k] = ahead[k]
            to_z[ct, 1, k] = behind[k]
        for r in (2, 1, 3):
            pl.when(z < NZ - 1)(lambda ct=ct, r=r: start_z(ct, r, 0).start())
            pl.when(lax.rem(z + r, NZ) < z)(lambda ct=ct, r=r: start_z(ct, r, 1).start())

    to_owners(sys_, syr, lines_recv.at[0])

    def stretches(m):
        wait_for(sxr.at[pl.ds(0, 2)], chip_recv.at[m])
        return columns(sxr[2 * m]) + columns(sxr[2 * m + 1])

    def left(m, _):
        rates = stretches(m)
        for ct in range(CT):
            for k, value in enumerate(transfer(rates, inverse_x[:, lanes(ct)], False)):
                chips[m, ct, k] = value
        return 0

    def right(m, _):
        rates = stretches(m)
        for ct in range(CT):
            t, g = transfer(rates, inverse_x[:, lanes(ct)], True)
            for k, value in enumerate(t + g):
                chips[m, ct, k] = value
        return 0

    lax.fori_loop(0, z, left, 0)
    lax.fori_loop(z + 1, NZ, right, 0)

    for ct in range(CT):
        for chip_z, messages in enumerate((5, 4, 3, 3)):
            pl.when(z == chip_z)(lambda ct=ct, messages=messages: wait_for(
                from_z.at[ct].reshape(2 * NZ, 4, 8, W).at[pl.ds(0, messages)], z_recv.at[ct]))

        def chip(m):
            return [chips[m, ct, k] for k in range(4)]

        def came(m, kind):
            return [from_z[ct, m, kind, k] for k in range(4)]

        def ahead(m, s):
            return toeplitz(chip(m), s, came(m, 0))

        def onward(m, s):
            s = ahead(m, s)
            for k in range(4):
                passing[ct, m + 1, k] = s[k]
            return s

        def behind(i, b):
            m = NZ - 1 - i
            g = [chips[m, ct, 4 + n] for n in range(10)]
            return toeplitz(chip(m), b, reflect(g, [passing[ct, m, k] for k in range(4)], came(m, 1)))

        s0 = lax.fori_loop(0, z, ahead, nothing)
        t0, t1, g1, (e0, e1) = blocks(ct)
        s1 = toeplitz(t0, s0, e0[:4])
        s2 = toeplitz(t1, s1, e1[:4])
        for k in range(4):
            passing[ct, z + 1, k] = s2[k]
        lax.fori_loop(z + 1, NZ - 1, onward, s2)
        b1 = lax.fori_loop(0, NZ - 1 - z, behind, nothing)
        b0 = toeplitz(t1, b1, reflect(g1, s1, e1[4:]))
        for b, states in enumerate([s0 + b0, s1 + b1]):
            for k in range(8):
                back[ct, b, k] = states[k]
        remote(back.at[ct, 1 - core], entering.at[ct, core], sent.at[0], back_recv.at[ct], other).start()
        entering[ct, core] = back[ct, core]

    for i in range(B):
        for ct in range(CT):
            py[ct, pl.ds(i * B, B), :] = jnp.exp(rate_y[:, i:i + 1] * inverse_y[:, lanes(ct)])

    for ct in range(CT):
        wait_for(entering.at[ct, 0], back_recv.at[ct])
        states = [jnp.concatenate([entering[ct, half, k] for half in range(2)], axis=0) for k in range(8)]

        def keep(i, w):
            u[ct, along(i), :] = w

        sweep(u.at[ct], px.at[ct], mid.at[ct], along, states[:4], states[4:], keep)
        ends = sweep(u.at[ct], py.at[ct], mid.at[ct], across, zeros, zeros)
        flat = ys1.at[ct].reshape(NY * 8, W)
        for k in range(8):
            for l in range(2):
                flat[pl.ds(64 * l + k, 8, stride=8), :] = ends[k][8 * l:8 * l + 8]
        to_owners(ys1.at[ct], yr1.at[ct], gather_recv.at[ct, core])

    @pl.when(core == 1)
    def _():
        wait_for(syr.reshape(2 * NY, 8, W).at[pl.ds(0, 2 * NY - 1)], lines_recv.at[0])
        for b in (1, 0):
            rates = columns(syr.at[b].reshape(NY * 8, W)[pl.ds(0, NY, stride=8), 0:B])
            for ct in range(CT):
                t, g = transfer(rates, inverse_y[:, lanes(ct)], True)
                flat = tgy.at[b, ct].reshape(NY * 16, W)
                for k, value in enumerate(t + g):
                    for l in range(2):
                        flat[pl.ds(128 * l + k, 8, stride=16), :] = value[8 * l:8 * l + 8]
        for ct in range(CT):
            for b in (1, 0):
                wait_for(yr1.at[ct, b, pl.ds(0, NY - b)], gather_recv.at[ct, b])
                chain(yr1.at[ct, b], tgy.at[b, ct], ys2.at[ct, b])
                for offset in OFFSETS_Y:
                    peer = peer_y(*offset)
                    remote(ys2.at[ct, b, peer], yr2.at[ct, gy], y_sent.at[0], reply_recv.at[ct],
                           (owner - 1 + b, peer)).start()
                if b == 0:
                    remote(ys2.at[ct, 0, gy], yr2.at[ct, gy], y_sent.at[0], reply_recv.at[ct], (owner - 1, gy)).start()
                else:
                    yr2[ct, gy] = ys2[ct, 1, gy]

    amplitude = 10.0 * jnp.minimum(reach, 0.25) * math.sqrt(NX * B * NY * B)
    for ct in range(CT):
        for b in range(2):
            pl.when(core == b)(lambda ct=ct, b=b: wait_for(yr2.at[ct, pl.ds(0, NY - b)], reply_recv.at[ct]))
        flat = yr2.at[ct].reshape(NY * 8, W)
        states = [flat[pl.ds(k, NY, stride=8), :] for k in range(8)]

        def finish(i, w):
            u[ct, across(i), :] = w * amplitude[:, lanes(ct)]

        sweep(u.at[ct], py.at[ct], mid.at[ct], across, states[:4], states[4:], finish)
        out[:, lanes(ct)] = u[ct]

    tiles = chips.reshape(NZ * CT * 14, 8, W)
    wait_for(tiles.at[pl.ds(0, NX - 1 + 16 * CT)], sent.at[0])
    for chip_z, messages in enumerate((3, 4, 5, 3)):
        pl.when(z == chip_z)(lambda messages=messages: wait_for(tiles.at[pl.ds(0, 4 * CT * messages)], z_sent.at[0]))
    for b, messages in enumerate(((CT + 1) * NY, (CT + 1) * (NY - 1) + CT * (2 * NY - 1))):
        pl.when(core == b)(lambda messages=messages: wait_for(tiles.at[pl.ds(0, messages)], y_sent.at[0]))


def shards(increment, vertical, col_reach, stretch_x, stretch_y):
    f32 = jnp.float32
    field = pltpu.VMEM((CT, B * B, W), f32)

    def states(*lead):
        return pltpu.VMEM(lead + (8, W), f32)

    def dma(*shape):
        return pltpu.SemaphoreType.DMA(shape)

    two, lines, both = states(CT, 2, 8), states(CT, NY), states(CT, 2, NY)
    operands = (increment.reshape(B * B, C), vertical, col_reach, stretch_x, stretch_y)
    result = pl.pallas_call(
        kernel,
        out_shape=jax.ShapeDtypeStruct((B * B, C), f32),
        in_specs=[pl.BlockSpec(memory_space=pltpu.HBM)] * 5,
        out_specs=pl.BlockSpec(memory_space=pltpu.VMEM),
        scratch_shapes=[
            pltpu.VMEM((B * B, C), jnp.bfloat16), pltpu.VMEM((C, C), jnp.bfloat16), pltpu.VMEM((C,), f32),
            pltpu.VMEM((B, B), f32), pltpu.VMEM((B, B), f32), dma(5),
            field, field, field, field,
            two, two, states(CT, 18), states(NZ, CT, 14), states(CT, NZ + 1, 4),
            states(CT, 2, 4), states(CT, NZ, 2, 4), two, two,
            lines, both, both, lines, pltpu.VMEM((2, CT, NY, 16, W), f32),
            states(2), states(NX), states(NY), states(2, NY),
            dma(1), dma(1), dma(1), dma(1), dma(NZ), dma(1), dma(CT),
            dma(CT), dma(CT), dma(CT, 2), dma(CT),
        ],
        compiler_params=pltpu.CompilerParams(
            collective_id=0, has_side_effects=True, vmem_limit_bytes=32 * 2**20),
        name="covariance",
    )(*[pltpu.with_memory_space_constraint(x, pltpu.HBM) for x in operands])
    return result.reshape(B, B, C)


def solution(mesh):
    in_specs = (P("gx", "gy", None), P(), P(), P("gx", "gy"), P("gx", "gy"))
    out_specs = P("gx", "gy", None)
    return jax.shard_map(shards, mesh=mesh, in_specs=in_specs, out_specs=out_specs, check_vma=False)
```

```python
import functools
import math

import jax
import jax.numpy as jnp
from jax import lax
from jax.experimental import pallas as pl
from jax.experimental.pallas import tpu as pltpu
from jax.sharding import PartitionSpec as P

MESH = pl.DeviceIdType.MESH
B = 16
NX, NY, NZ = 8, 16, 4
C, W, CT = 384, 128, 3
OFFSETS_Y = sorted([(a, b) for a in range(4) for b in range(4) if a or b],
                   key=lambda o: -min(o[0], 4 - o[0]) - min(o[1], 4 - o[1]))
PAIRS = [(a, b) for a in range(4) for b in range(a, 4)]


def cascade(state, u, p, q):
    out = []
    for k in range(4):
        u = p * state[k] + q * u
        out.append(u)
    return out, u


def toeplitz(t, s, add):
    out = []
    for k in range(4):
        total = add[k]
        for m in range(k + 1):
            total = total + t[k - m] * s[m]
        out.append(total)
    return out


def reflect(g, s, add):
    out = []
    for a in range(4):
        total = add[a]
        for m in range(4):
            total = total + g[PAIRS.index((min(a, 3 - m), max(a, 3 - m)))] * s[m]
        out.append(total)
    return out


def transfer(rates, scale, reflecting):
    c, g = None, [None] * 10
    for rate in rates:
        p = jnp.exp(rate * scale)
        q = 1.0 - p
        if c is None:
            d = [jnp.ones_like(p), q]
            d.append(q * d[1])
            d.append(q * d[2])
        else:
            d = [c[0]]
            for k in range(1, 4):
                d.append(c[k] + q * d[k - 1])
        c = [p * x for x in d]
        if reflecting:
            e = [q * x for x in c]
            for n, (a, b) in enumerate(PAIRS):
                term = d[a] * e[b]
                g[n] = term if g[n] is None else g[n] + term
    return (c, g) if reflecting else c


def columns(tile):
    return [tile[:, i:i + 1] for i in range(B)]


def sweep(source, poles, mid, rows_of, first, second, sink=None):
    state = first
    for i in range(B):
        rows = pl.ds(i * B, B)
        p = poles[rows, :]
        state, w = cascade(state, source[rows_of(i), :], p, 1.0 - p)
        mid[rows, :] = w
    ahead, state = state, second
    for i in reversed(range(B)):
        rows = pl.ds(i * B, B)
        p = poles[rows, :]
        state, w = cascade(state, mid[rows, :], p, 1.0 - p)
        if sink is not None:
            sink(i, w)
    return ahead + state


def chain(got, coefs, reply):
    zero = [jnp.zeros((1, W), jnp.float32)] * 4

    def at(ref, j, k):
        return ref[j, k:k + 1, :]

    s, entered = zero, []
    for j in range(NY):
        entered.append(s)
        for k in range(4):
            reply[j, k:k + 1, :] = s[k]
        s = toeplitz([at(coefs, j, k) for k in range(4)], s, [at(got, j, k) for k in range(4)])
    b = zero
    for j in reversed(range(NY)):
        for k in range(4):
            reply[j, 4 + k:5 + k, :] = b[k]
        g = [at(coefs, j, 4 + n) for n in range(10)]
        add = reflect(g, entered[j], [at(got, j, 4 + k) for k in range(4)])
        b = toeplitz([at(coefs, j, k) for k in range(4)], b, add)


def kernel(inc_hbm, vert_hbm, reach_hbm, sx_hbm, sy_hbm, out,
           inc, vert, reach_line, sx, sy, load_sem, u, px, py, mid,
           ends_x, pair, own, chips, passing, to_z, from_z, back, entering, ys1, yr1, ys2, yr2,
           tgy, sxs, sxr, sys_, syr, sent, z_sent, y_sent, beside_recv, chip_recv, lines_recv, pair_recv,
           z_recv, back_recv, gather_recv, reply_recv):
    gx, gy = lax.axis_index("gx"), lax.axis_index("gy")
    z, core = gx // 2, lax.rem(gx, 2)
    other = (gx + 1 - 2 * core, gy)
    owner = 2 * z + 1

    def peer_y(dy, dx):
        return lax.rem(gy // 4 + dy, 4) * 4 + lax.rem(gy + dx, 4)

    barrier = pltpu.get_barrier_semaphore()
    for r in range(1, NX):
        pl.semaphore_signal(barrier, inc=1, device_id=(lax.rem(gx + r, NX), gy), device_id_type=MESH)
    for offset in OFFSETS_Y:
        pl.semaphore_signal(barrier, inc=1, device_id=(owner, peer_y(*offset)), device_id_type=MESH)

    @pl.when(core == 1)
    def _():
        for offset in OFFSETS_Y:
            pl.semaphore_signal(barrier, inc=1, device_id=(owner - 1, peer_y(*offset)), device_id_type=MESH)

    loads = [pltpu.make_async_copy(src, dst, load_sem.at[n]) for n, (src, dst) in enumerate(
        [(sx_hbm, sx), (reach_hbm, reach_line), (vert_hbm, vert), (inc_hbm, inc), (sy_hbm, sy)])]
    for load in loads:
        load.start()

    def remote(src, dst, sent, got, device):
        return pltpu.make_async_remote_copy(src, dst, sent, got, device_id=device, device_id_type=MESH)

    def to_owners(src, dst, got):
        for offset in OFFSETS_Y:
            peer = peer_y(*offset)
            remote(src.at[peer], dst.at[core, gy], y_sent.at[0], got, (owner, peer)).start()

        @pl.when(core == 0)
        def _():
            remote(src.at[gy], dst.at[0, gy], y_sent.at[0], got, (owner, gy)).start()

        @pl.when(core == 1)
        def _():
            dst[1, gy] = src[gy]

    def wait_for(part, sem):
        pltpu.make_async_copy(part, part, sem).wait()

    def lanes(ct):
        return slice(ct * W, (ct + 1) * W)

    loads[0].wait()
    loads[1].wait()
    reach = reach_line[...].reshape(1, C)
    rate_x = -1.0 / sx[...].T
    inverse_x = 1.0 / (reach * float(NX * B))
    inverse_y = 1.0 / (reach * float(NY * B))
    for i in range(B):
        for ct in range(CT):
            px[ct, pl.ds(i * B, B), :] = jnp.exp(rate_x[:, i:i + 1] * inverse_x[:, lanes(ct)])
    loads[4].wait()
    rate_y = -1.0 / sy[...]
    for half in range(2):
        sxs[half, :, 0:B] = rate_x[8 * half:8 * half + 8]
        sys_.reshape(NY * 8, W)[pl.ds(64 * half, 8, stride=8), 0:B] = rate_y[8 * half:8 * half + 8]
    loads[2].wait()
    loads[3].wait()
    mixed = jnp.dot(inc[...], vert[...], preferred_element_type=jnp.float32)
    for ct in range(CT):
        u[ct] = mixed[:, lanes(ct)]

    zeros = [jnp.zeros((B, W), jnp.float32)] * 4
    nothing = [jnp.zeros((8, W), jnp.float32)] * 4

    def along(i):
        return pl.ds(i * B, B)

    def across(i):
        return pl.ds(i, B, stride=B)

    for ct in range(CT):
        ends = sweep(u.at[ct], px.at[ct], mid.at[ct], along, zeros, zeros)
        for half in range(2):
            for k in range(8):
                ends_x[ct, half, k] = ends[k][8 * half:8 * half + 8]

    pl.semaphore_wait(barrier, NX + NY - 2 + core * (NY - 1))
    remote(sxs.at[1 - core], sxr.at[gx], sent.at[0], beside_recv.at[0], other).start()
    for r in (2, 1, 3):
        for c in range(2):
            peer = 2 * lax.rem(z + r, NZ) + c
            remote(sxs.at[c], sxr.at[gx], sent.at[0], chip_recv.at[z], (peer, gy)).start()
    for ct in range(CT):
        remote(ends_x.at[ct, 1 - core], pair.at[ct, core], sent.at[0], pair_recv.at[ct], other).start()
    sxr[gx] = sxs[core]
    for ct in range(CT):
        pair[ct, core] = ends_x[ct, core]

    def start_z(ct, r, kind):
        peer = lax.rem(z + r, NZ)
        return remote(to_z.at[ct, kind], from_z.at[ct, z, kind], z_sent.at[0], z_recv.at[ct],
                      (2 * peer + core, gy))

    def blocks(ct):
        t0, t1 = [own[ct, k] for k in range(4)], [own[ct, 4 + k] for k in range(4)]
        g1 = [own[ct, 8 + n] for n in range(10)]
        return t0, t1, g1, [[pair[ct, b, k] for k in range(8)] for b in range(2)]

    wait_for(sxr.at[0], beside_recv.at[0])
    first, second = columns(sxr[2 * z]), columns(sxr[2 * z + 1])
    for ct in range(CT):
        scale = inverse_x[:, lanes(ct)]
        t, g = transfer(second, scale, True)
        for k, value in enumerate(transfer(first, scale, False) + t + g):
            own[ct, k] = value
        wait_for(pair.at[ct, 0], pair_recv.at[ct])
        t0, t1, g1, (e0, e1) = blocks(ct)
        ahead = toeplitz(t1, e0[:4], e1[:4])
        behind = toeplitz(t0, reflect(g1, e0[:4], e1[4:]), e0[4:])
        for k in range(4):
            to_z[ct, 0, k] = ahead[k]
            to_z[ct, 1, k] = behind[k]
        for r in (2, 1, 3):
            pl.when(z < NZ - 1)(lambda ct=ct, r=r: start_z(ct, r, 0).start())
            pl.when(lax.rem(z + r, NZ) < z)(lambda ct=ct, r=r: start_z(ct, r, 1).start())

    to_owners(sys_, syr, lines_recv.at[0])

    def stretches(m):
        wait_for(sxr.at[pl.ds(0, 2)], chip_recv.at[m])
        return columns(sxr[2 * m]) + columns(sxr[2 * m + 1])

    def left(m, _):
        rates = stretches(m)
        for ct in range(CT):
            for k, value in enumerate(transfer(rates, inverse_x[:, lanes(ct)], False)):
                chips[m, ct, k] = value
        return 0

    def right(m, _):
        rates = stretches(m)
        for ct in range(CT):
            t, g = transfer(rates, inverse_x[:, lanes(ct)], True)
            for k, value in enumerate(t + g):
                chips[m, ct, k] = value
        return 0

    lax.fori_loop(0, z, left, 0)
    lax.fori_loop(z + 1, NZ, right, 0)

    for ct in range(CT):
        for chip_z, messages in enumerate((5, 4, 3, 3)):
            pl.when(z == chip_z)(lambda ct=ct, messages=messages: wait_for(
                from_z.at[ct].reshape(2 * NZ, 4, 8, W).at[pl.ds(0, messages)], z_recv.at[ct]))

        def chip(m):
            return [chips[m, ct, k] for k in range(4)]

        def came(m, kind):
            return [from_z[ct, m, kind, k] for k in range(4)]

        def ahead(m, s):
            return toeplitz(chip(m), s, came(m, 0))

        def onward(m, s):
            s = ahead(m, s)
            for k in range(4):
                passing[ct, m + 1, k] = s[k]
            return s

        def behind(i, b):
            m = NZ - 1 - i
            g = [chips[m, ct, 4 + n] for n in range(10)]
            return toeplitz(chip(m), b, reflect(g, [passing[ct, m, k] for k in range(4)], came(m, 1)))

        s0 = lax.fori_loop(0, z, ahead, nothing)
        t0, t1, g1, (e0, e1) = blocks(ct)
        s1 = toeplitz(t0, s0, e0[:4])
        s2 = toeplitz(t1, s1, e1[:4])
        for k in range(4):
            passing[ct, z + 1, k] = s2[k]
        lax.fori_loop(z + 1, NZ - 1, onward, s2)
        b1 = lax.fori_loop(0, NZ - 1 - z, behind, nothing)
        b0 = toeplitz(t1, b1, reflect(g1, s1, e1[4:]))
        for b, states in enumerate([s0 + b0, s1 + b1]):
            for k in range(8):
                back[ct, b, k] = states[k]
        remote(back.at[ct, 1 - core], entering.at[ct, core], sent.at[0], back_recv.at[ct], other).start()
        entering[ct, core] = back[ct, core]

    for i in range(B):
        for ct in range(CT):
            py[ct, pl.ds(i * B, B), :] = jnp.exp(rate_y[:, i:i + 1] * inverse_y[:, lanes(ct)])

    for ct in range(CT):
        wait_for(entering.at[ct, 0], back_recv.at[ct])
        states = [jnp.concatenate([entering[ct, half, k] for half in range(2)], axis=0) for k in range(8)]

        def keep(i, w):
            u[ct, along(i), :] = w

        sweep(u.at[ct], px.at[ct], mid.at[ct], along, states[:4], states[4:], keep)
        ends = sweep(u.at[ct], py.at[ct], mid.at[ct], across, zeros, zeros)
        flat = ys1.at[ct].reshape(NY * 8, W)
        for k in range(8):
            for l in range(2):
                flat[pl.ds(64 * l + k, 8, stride=8), :] = ends[k][8 * l:8 * l + 8]
        to_owners(ys1.at[ct], yr1.at[ct], gather_recv.at[ct, core])

    @pl.when(core == 1)
    def _():
        wait_for(syr.reshape(2 * NY, 8, W).at[pl.ds(0, 2 * NY - 1)], lines_recv.at[0])
        for b in (1, 0):
            rates = columns(syr.at[b].reshape(NY * 8, W)[pl.ds(0, NY, stride=8), 0:B])
            for ct in range(CT):
                t, g = transfer(rates, inverse_y[:, lanes(ct)], True)
                flat = tgy.at[b, ct].reshape(NY * 16, W)
                for k, value in enumerate(t + g):
                    for l in range(2):
                        flat[pl.ds(128 * l + k, 8, stride=16), :] = value[8 * l:8 * l + 8]
        for b in (1, 0):
            for ct in range(CT):
                wait_for(yr1.at[ct, b, pl.ds(0, NY - b)], gather_recv.at[ct, b])
                chain(yr1.at[ct, b], tgy.at[b, ct], ys2.at[ct, b])
                for offset in OFFSETS_Y:
                    peer = peer_y(*offset)
                    remote(ys2.at[ct, b, peer], yr2.at[ct, gy], y_sent.at[0], reply_recv.at[ct],
                           (owner - 1 + b, peer)).start()
                if b == 0:
                    remote(ys2.at[ct, 0, gy], yr2.at[ct, gy], y_sent.at[0], reply_recv.at[ct], (owner - 1, gy)).start()
                else:
                    yr2[ct, gy] = ys2[ct, 1, gy]

    amplitude = 10.0 * jnp.minimum(reach, 0.25) * math.sqrt(NX * B * NY * B)
    for ct in range(CT):
        for b in range(2):
            pl.when(core == b)(lambda ct=ct, b=b: wait_for(yr2.at[ct, pl.ds(0, NY - b)], reply_recv.at[ct]))
        flat = yr2.at[ct].reshape(NY * 8, W)
        states = [flat[pl.ds(k, NY, stride=8), :] for k in range(8)]

        def finish(i, w):
            u[ct, across(i), :] = w * amplitude[:, lanes(ct)]

        sweep(u.at[ct], py.at[ct], mid.at[ct], across, states[:4], states[4:], finish)
        out[:, lanes(ct)] = u[ct]

    tiles = chips.reshape(NZ * CT * 14, 8, W)
    wait_for(tiles.at[pl.ds(0, NX - 1 + 16 * CT)], sent.at[0])
    for chip_z, messages in enumerate((3, 4, 5, 3)):
        pl.when(z == chip_z)(lambda messages=messages: wait_for(tiles.at[pl.ds(0, 4 * CT * messages)], z_sent.at[0]))
    for b, messages in enumerate(((CT + 1) * NY, (CT + 1) * (NY - 1) + CT * (2 * NY - 1))):
        pl.when(core == b)(lambda messages=messages: wait_for(tiles.at[pl.ds(0, messages)], y_sent.at[0]))


def shards(increment, vertical, col_reach, stretch_x, stretch_y):
    f32 = jnp.float32
    field = pltpu.VMEM((CT, B * B, W), f32)

    def states(*lead):
        return pltpu.VMEM(lead + (8, W), f32)

    def dma(*shape):
        return pltpu.SemaphoreType.DMA(shape)

    two, lines, both = states(CT, 2, 8), states(CT, NY), states(CT, 2, NY)
    operands = (increment.reshape(B * B, C), vertical, col_reach, stretch_x, stretch_y)
    result = pl.pallas_call(
        kernel,
        out_shape=jax.ShapeDtypeStruct((B * B, C), f32),
        in_specs=[pl.BlockSpec(memory_space=pltpu.HBM)] * 5,
        out_specs=pl.BlockSpec(memory_space=pltpu.VMEM),
        scratch_shapes=[
            pltpu.VMEM((B * B, C), jnp.bfloat16), pltpu.VMEM((C, C), jnp.bfloat16), pltpu.VMEM((C,), f32),
            pltpu.VMEM((B, B), f32), pltpu.VMEM((B, B), f32), dma(5),
            field, field, field, field,
            two, two, states(CT, 18), states(NZ, CT, 14), states(CT, NZ + 1, 4),
            states(CT, 2, 4), states(CT, NZ, 2, 4), two, two,
            lines, both, both, lines, pltpu.VMEM((2, CT, NY, 16, W), f32),
            states(2), states(NX), states(NY), states(2, NY),
            dma(1), dma(1), dma(1), dma(1), dma(NZ), dma(1), dma(CT),
            dma(CT), dma(CT), dma(CT, 2), dma(CT),
        ],
        compiler_params=pltpu.CompilerParams(
            collective_id=0, has_side_effects=True, vmem_limit_bytes=32 * 2**20),
        name="covariance",
    )(*[pltpu.with_memory_space_constraint(x, pltpu.HBM) for x in operands])
    return result.reshape(B, B, C)


def solution(mesh):
    in_specs = (P("gx", "gy", None), P(), P(), P("gx", "gy"), P("gx", "gy"))
    out_specs = P("gx", "gy", None)
    return jax.shard_map(shards, mesh=mesh, in_specs=in_specs, out_specs=out_specs, check_vma=False)
```

```python
import functools
import math

import jax
import jax.numpy as jnp
from jax import lax
from jax.experimental import pallas as pl
from jax.experimental.pallas import tpu as pltpu
from jax.sharding import PartitionSpec as P

MESH = pl.DeviceIdType.MESH
B = 16
NX, NY, NZ = 8, 16, 4
C, W, CT = 384, 128, 3
OFFSETS_Y = sorted([(a, b) for a in range(4) for b in range(4) if a or b],
                   key=lambda o: -min(o[0], 4 - o[0]) - min(o[1], 4 - o[1]))
ORDER = ((1, 0), (1, 1), (0, 0), (1, 2), (0, 1), (0, 2))
PAIRS = [(a, b) for a in range(4) for b in range(a, 4)]


def cascade(state, u, p, q):
    out = []
    for k in range(4):
        u = p * state[k] + q * u
        out.append(u)
    return out, u


def toeplitz(t, s, add):
    out = []
    for k in range(4):
        total = add[k]
        for m in range(k + 1):
            total = total + t[k - m] * s[m]
        out.append(total)
    return out


def reflect(g, s, add):
    out = []
    for a in range(4):
        total = add[a]
        for m in range(4):
            total = total + g[PAIRS.index((min(a, 3 - m), max(a, 3 - m)))] * s[m]
        out.append(total)
    return out


def poles(stretch, scale):
    return jnp.exp(-1.0 / (stretch * scale))


def transfer(stretches, scale, reflecting):
    c, g = None, [None] * 10
    for stretch in stretches:
        p = poles(stretch, scale)
        q = 1.0 - p
        if c is None:
            d = [jnp.ones_like(p), q]
            d.append(q * d[1])
            d.append(q * d[2])
        else:
            d = [c[0]]
            for k in range(1, 4):
                d.append(c[k] + q * d[k - 1])
        c = [p * x for x in d]
        if reflecting:
            e = [q * x for x in c]
            for n, (a, b) in enumerate(PAIRS):
                term = d[a] * e[b]
                g[n] = term if g[n] is None else g[n] + term
    return (c, g) if reflecting else c


def columns(tile):
    return [tile[:, i:i + 1] for i in range(B)]


def sweep(source, pole, mid, rows_of, first, second, sink=None):
    state = first
    for i in range(B):
        rows = pl.ds(i * B, B)
        p = pole[rows, :]
        state, w = cascade(state, source[rows_of(i), :], p, 1.0 - p)
        mid[rows, :] = w
    ahead, state = state, second
    for i in reversed(range(B)):
        rows = pl.ds(i * B, B)
        p = pole[rows, :]
        state, w = cascade(state, mid[rows, :], p, 1.0 - p)
        if sink is not None:
            sink(i, w)
    return ahead + state


def chain(got, coefs, reply):
    zero = [jnp.zeros((1, W), jnp.float32)] * 4

    def at(ref, j, k):
        return ref[j, k:k + 1, :]

    s, entered = zero, []
    for j in range(NY):
        entered.append(s)
        for k in range(4):
            reply[j, k:k + 1, :] = s[k]
        s = toeplitz([at(coefs, j, k) for k in range(4)], s, [at(got, j, k) for k in range(4)])
    b = zero
    for j in reversed(range(NY)):
        for k in range(4):
            reply[j, 4 + k:5 + k, :] = b[k]
        g = [at(coefs, j, 4 + n) for n in range(10)]
        add = reflect(g, entered[j], [at(got, j, 4 + k) for k in range(4)])
        b = toeplitz([at(coefs, j, k) for k in range(4)], b, add)


def kernel(inc_hbm, vert_hbm, reach_hbm, sx_hbm, sy_hbm, out,
           inc, vert, reach_line, sx, sy, load_sem, u, px, py, mid,
           ends_x, pair, own, chips, passing, to_z, from_z, back, entering, ys1, yr1, ys2, yr2,
           tgy, sxs, sxr, sys_, syr, sent, z_sent, y_sent, beside_recv, chip_recv, lines_recv, pair_recv,
           z_recv, back_recv, gather_recv, reply_recv):
    gx, gy = lax.axis_index("gx"), lax.axis_index("gy")
    z, core = gx // 2, lax.rem(gx, 2)
    other = (gx + 1 - 2 * core, gy)
    owner = 2 * z + 1

    def peer_y(dy, dx):
        return lax.rem(gy // 4 + dy, 4) * 4 + lax.rem(gy + dx, 4)

    barrier = pltpu.get_barrier_semaphore()
    for r in range(1, NX):
        pl.semaphore_signal(barrier, inc=1, device_id=(lax.rem(gx + r, NX), gy), device_id_type=MESH)
    for offset in OFFSETS_Y:
        pl.semaphore_signal(barrier, inc=1, device_id=(owner, peer_y(*offset)), device_id_type=MESH)

    @pl.when(core == 1)
    def _():
        for offset in OFFSETS_Y:
            pl.semaphore_signal(barrier, inc=1, device_id=(owner - 1, peer_y(*offset)), device_id_type=MESH)

    loads = [pltpu.make_async_copy(src, dst, load_sem.at[n]) for n, (src, dst) in enumerate(
        [(sx_hbm, sx), (reach_hbm, reach_line), (vert_hbm, vert), (inc_hbm, inc), (sy_hbm, sy)])]
    for load in loads:
        load.start()

    def remote(src, dst, sent, got, device):
        return pltpu.make_async_remote_copy(src, dst, sent, got, device_id=device, device_id_type=MESH)

    def to_owners(src, dst, got):
        for offset in OFFSETS_Y:
            peer = peer_y(*offset)
            remote(src.at[peer], dst.at[core, gy], y_sent.at[0], got, (owner, peer)).start()

        @pl.when(core == 0)
        def _():
            remote(src.at[gy], dst.at[0, gy], y_sent.at[0], got, (owner, gy)).start()

        @pl.when(core == 1)
        def _():
            dst[1, gy] = src[gy]

    def wait_for(part, sem):
        pltpu.make_async_copy(part, part, sem).wait()

    def lanes(ct):
        return slice(ct * W, (ct + 1) * W)

    loads[0].wait()
    loads[1].wait()
    reach = reach_line[...].reshape(1, C)
    stretch_x = sx[...].T
    scale_x = reach * float(NX * B)
    scale_y = reach * float(NY * B)
    for i in range(B):
        for ct in range(CT):
            px[ct, pl.ds(i * B, B), :] = poles(stretch_x[:, i:i + 1], scale_x[:, lanes(ct)])
    loads[4].wait()
    stretch_y = sy[...]
    for half in range(2):
        sxs[half, :, 0:B] = stretch_x[8 * half:8 * half + 8]
        sys_.reshape(NY * 8, W)[pl.ds(64 * half, 8, stride=8), 0:B] = stretch_y[8 * half:8 * half + 8]
    loads[2].wait()
    loads[3].wait()
    mixed = jnp.dot(inc[...], vert[...], preferred_element_type=jnp.float32)
    for ct in range(CT):
        u[ct] = mixed[:, lanes(ct)]

    zeros = [jnp.zeros((B, W), jnp.float32)] * 4
    nothing = [jnp.zeros((8, W), jnp.float32)] * 4

    def along(i):
        return pl.ds(i * B, B)

    def across(i):
        return pl.ds(i, B, stride=B)

    for ct in range(CT):
        ends = sweep(u.at[ct], px.at[ct], mid.at[ct], along, zeros, zeros)
        for half in range(2):
            for k in range(8):
                ends_x[ct, half, k] = ends[k][8 * half:8 * half + 8]

    pl.semaphore_wait(barrier, NX + NY - 2 + core * (NY - 1))
    remote(sxs.at[1 - core], sxr.at[gx], sent.at[0], beside_recv.at[0], other).start()
    for r in (2, 1, 3):
        for c in range(2):
            peer = 2 * lax.rem(z + r, NZ) + c
            remote(sxs.at[c], sxr.at[gx], sent.at[0], chip_recv.at[z], (peer, gy)).start()
    for ct in range(CT):
        remote(ends_x.at[ct, 1 - core], pair.at[ct, core], sent.at[0], pair_recv.at[ct], other).start()
    sxr[gx] = sxs[core]
    for ct in range(CT):
        pair[ct, core] = ends_x[ct, core]

    def start_z(ct, r, kind):
        peer = lax.rem(z + r, NZ)
        return remote(to_z.at[ct, kind], from_z.at[ct, z, kind], z_sent.at[0], z_recv.at[ct],
                      (2 * peer + core, gy))

    def blocks(ct):
        t0, t1 = [[own[ct, b, k] for k in range(4)] for b in range(2)]
        g1 = [own[ct, 1, 4 + n] for n in range(10)]
        return t0, t1, g1, [[pair[ct, b, k] for k in range(8)] for b in range(2)]

    def block_transfer(ct, b):
        t, g = transfer(columns(sxr[2 * z + b]), scale_x[:, lanes(ct)], True)
        for k, value in enumerate(t + g):
            own[ct, b, k] = value

    for ct in range(CT):
        block_transfer(ct, core)
    wait_for(sxr.at[0], beside_recv.at[0])
    for ct in range(CT):
        block_transfer(ct, 1 - core)
        wait_for(pair.at[ct, 0], pair_recv.at[ct])
        t0, t1, g1, (e0, e1) = blocks(ct)
        ahead = toeplitz(t1, e0[:4], e1[:4])
        behind = toeplitz(t0, reflect(g1, e0[:4], e1[4:]), e0[4:])
        for k in range(4):
            to_z[ct, 0, k] = ahead[k]
            to_z[ct, 1, k] = behind[k]
        for r in (2, 1, 3):
            pl.when(z < NZ - 1)(lambda ct=ct, r=r: start_z(ct, r, 0).start())
            pl.when(lax.rem(z + r, NZ) < z)(lambda ct=ct, r=r: start_z(ct, r, 1).start())

    to_owners(sys_, syr, lines_recv.at[0])

    def stretches(m):
        wait_for(sxr.at[pl.ds(0, 2)], chip_recv.at[m])
        return columns(sxr[2 * m]) + columns(sxr[2 * m + 1])

    def left(m, _):
        rates = stretches(m)
        for ct in range(CT):
            for k, value in enumerate(transfer(rates, scale_x[:, lanes(ct)], False)):
                chips[m, ct, k] = value
        return 0

    def right(m, _):
        rates = stretches(m)
        for ct in range(CT):
            t, g = transfer(rates, scale_x[:, lanes(ct)], True)
            for k, value in enumerate(t + g):
                chips[m, ct, k] = value
        return 0

    lax.fori_loop(0, z, left, 0)
    lax.fori_loop(z + 1, NZ, right, 0)
    for i in range(B):
        for ct in range(CT):
            py[ct, pl.ds(i * B, B), :] = poles(stretch_y[:, i:i + 1], scale_y[:, lanes(ct)])

    for ct in range(CT):
        for chip_z, messages in enumerate((5, 4, 3, 3)):
            pl.when(z == chip_z)(lambda ct=ct, messages=messages: wait_for(
                from_z.at[ct].reshape(2 * NZ, 4, 8, W).at[pl.ds(0, messages)], z_recv.at[ct]))

        def chip(m):
            return [chips[m, ct, k] for k in range(4)]

        def came(m, kind):
            return [from_z[ct, m, kind, k] for k in range(4)]

        def ahead(m, s):
            return toeplitz(chip(m), s, came(m, 0))

        def onward(m, s):
            s = ahead(m, s)
            for k in range(4):
                passing[ct, m + 1, k] = s[k]
            return s

        def behind(i, b):
            m = NZ - 1 - i
            g = [chips[m, ct, 4 + n] for n in range(10)]
            return toeplitz(chip(m), b, reflect(g, [passing[ct, m, k] for k in range(4)], came(m, 1)))

        s0 = lax.fori_loop(0, z, ahead, nothing)
        t0, t1, g1, (e0, e1) = blocks(ct)
        s1 = toeplitz(t0, s0, e0[:4])
        s2 = toeplitz(t1, s1, e1[:4])
        for k in range(4):
            passing[ct, z + 1, k] = s2[k]
        lax.fori_loop(z + 1, NZ - 1, onward, s2)
        b1 = lax.fori_loop(0, NZ - 1 - z, behind, nothing)
        b0 = toeplitz(t1, b1, reflect(g1, s1, e1[4:]))
        for b, states in enumerate([s0 + b0, s1 + b1]):
            for k in range(8):
                back[ct, b, k] = states[k]
        remote(back.at[ct, 1 - core], entering.at[ct, core], sent.at[0], back_recv.at[ct], other).start()
        entering[ct, core] = back[ct, core]


    for ct in range(CT):
        wait_for(entering.at[ct, 0], back_recv.at[ct])
        states = [jnp.concatenate([entering[ct, half, k] for half in range(2)], axis=0) for k in range(8)]

        def keep(i, w):
            u[ct, along(i), :] = w

        sweep(u.at[ct], px.at[ct], mid.at[ct], along, states[:4], states[4:], keep)
        ends = sweep(u.at[ct], py.at[ct], mid.at[ct], across, zeros, zeros)
        flat = ys1.at[ct].reshape(NY * 8, W)
        for k in range(8):
            for l in range(2):
                flat[pl.ds(64 * l + k, 8, stride=8), :] = ends[k][8 * l:8 * l + 8]
        to_owners(ys1.at[ct], yr1.at[ct], gather_recv.at[ct, core])

    @pl.when(core == 1)
    def _():
        wait_for(syr.reshape(2 * NY, 8, W).at[pl.ds(0, 2 * NY - 1)], lines_recv.at[0])
        for b in (1, 0):
            rates = columns(syr.at[b].reshape(NY * 8, W)[pl.ds(0, NY, stride=8), 0:B])
            for ct in range(CT):
                t, g = transfer(rates, scale_y[:, lanes(ct)], True)
                flat = tgy.at[b, ct].reshape(NY * 16, W)
                for k, value in enumerate(t + g):
                    for l in range(2):
                        flat[pl.ds(128 * l + k, 8, stride=16), :] = value[8 * l:8 * l + 8]
        for b, ct in ORDER:
            wait_for(yr1.at[ct, b, pl.ds(0, NY - b)], gather_recv.at[ct, b])
            chain(yr1.at[ct, b], tgy.at[b, ct], ys2.at[ct, b])
            for offset in OFFSETS_Y:
                peer = peer_y(*offset)
                remote(ys2.at[ct, b, peer], yr2.at[ct, gy], y_sent.at[0], reply_recv.at[ct],
                       (owner - 1 + b, peer)).start()
            if b == 0:
                remote(ys2.at[ct, 0, gy], yr2.at[ct, gy], y_sent.at[0], reply_recv.at[ct], (owner - 1, gy)).start()
            else:
                yr2[ct, gy] = ys2[ct, 1, gy]

    amplitude = 10.0 * jnp.minimum(reach, 0.25) * math.sqrt(NX * B * NY * B)
    for ct in range(CT):
        for b in range(2):
            pl.when(core == b)(lambda ct=ct, b=b: wait_for(yr2.at[ct, pl.ds(0, NY - b)], reply_recv.at[ct]))
        flat = yr2.at[ct].reshape(NY * 8, W)
        states = [flat[pl.ds(k, NY, stride=8), :] for k in range(8)]

        def finish(i, w):
            u[ct, across(i), :] = w * amplitude[:, lanes(ct)]

        sweep(u.at[ct], py.at[ct], mid.at[ct], across, states[:4], states[4:], finish)
        out[:, lanes(ct)] = u[ct]

    tiles = chips.reshape(NZ * CT * 14, 8, W)
    wait_for(tiles.at[pl.ds(0, NX - 1 + 16 * CT)], sent.at[0])
    for chip_z, messages in enumerate((3, 4, 5, 3)):
        pl.when(z == chip_z)(lambda messages=messages: wait_for(tiles.at[pl.ds(0, 4 * CT * messages)], z_sent.at[0]))
    for b, messages in enumerate(((CT + 1) * NY, (CT + 1) * (NY - 1) + CT * (2 * NY - 1))):
        pl.when(core == b)(lambda messages=messages: wait_for(tiles.at[pl.ds(0, messages)], y_sent.at[0]))


def shards(increment, vertical, col_reach, stretch_x, stretch_y):
    f32 = jnp.float32
    field = pltpu.VMEM((CT, B * B, W), f32)

    def states(*lead):
        return pltpu.VMEM(lead + (8, W), f32)

    def dma(*shape):
        return pltpu.SemaphoreType.DMA(shape)

    two, lines, both = states(CT, 2, 8), states(CT, NY), states(CT, 2, NY)
    operands = (increment.reshape(B * B, C), vertical, col_reach, stretch_x, stretch_y)
    result = pl.pallas_call(
        kernel,
        out_shape=jax.ShapeDtypeStruct((B * B, C), f32),
        in_specs=[pl.BlockSpec(memory_space=pltpu.HBM)] * 5,
        out_specs=pl.BlockSpec(memory_space=pltpu.VMEM),
        scratch_shapes=[
            pltpu.VMEM((B * B, C), jnp.bfloat16), pltpu.VMEM((C, C), jnp.bfloat16), pltpu.VMEM((C,), f32),
            pltpu.VMEM((B, B), f32), pltpu.VMEM((B, B), f32), dma(5),
            field, field, field, field,
            two, two, states(CT, 2, 14), states(NZ, CT, 14), states(CT, NZ + 1, 4),
            states(CT, 2, 4), states(CT, NZ, 2, 4), two, two,
            lines, both, both, lines, pltpu.VMEM((2, CT, NY, 16, W), f32),
            states(2), states(NX), states(NY), states(2, NY),
            dma(1), dma(1), dma(1), dma(1), dma(NZ), dma(1), dma(CT),
            dma(CT), dma(CT), dma(CT, 2), dma(CT),
        ],
        compiler_params=pltpu.CompilerParams(
            collective_id=0, has_side_effects=True, vmem_limit_bytes=32 * 2**20),
        name="covariance",
    )(*[pltpu.with_memory_space_constraint(x, pltpu.HBM) for x in operands])
    return result.reshape(B, B, C)


def solution(mesh):
    in_specs = (P("gx", "gy", None), P(), P(), P("gx", "gy"), P("gx", "gy"))
    out_specs = P("gx", "gy", None)
    return jax.shard_map(shards, mesh=mesh, in_specs=in_specs, out_specs=out_specs, check_vma=False)
```

```python
import functools
import math

import jax
import jax.numpy as jnp
from jax import lax
from jax.experimental import pallas as pl
from jax.experimental.pallas import tpu as pltpu
from jax.sharding import PartitionSpec as P

MESH = pl.DeviceIdType.MESH
B = 16
NX, NY, NZ = 8, 16, 4
C, W, CT = 384, 128, 3
OFFSETS_Y = sorted([(a, b) for a in range(4) for b in range(4) if a or b],
                   key=lambda o: -min(o[0], 4 - o[0]) - min(o[1], 4 - o[1]))
ORDER = ((1, 0), (1, 1), (0, 0), (1, 2), (0, 1), (0, 2))
PAIRS = [(a, b) for a in range(4) for b in range(a, 4)]


def cascade(state, u, p, q):
    out = []
    for k in range(4):
        u = p * state[k] + q * u
        out.append(u)
    return out, u


def toeplitz(t, s, add):
    out = []
    for k in range(4):
        total = add[k]
        for m in range(k + 1):
            total = total + t[k - m] * s[m]
        out.append(total)
    return out


def reflect(g, s, add):
    out = []
    for a in range(4):
        total = add[a]
        for m in range(4):
            total = total + g[PAIRS.index((min(a, 3 - m), max(a, 3 - m)))] * s[m]
        out.append(total)
    return out


def poles(stretch, scale):
    return jnp.exp(-1.0 / (stretch * scale))


def transfer(stretches, scale, reflecting):
    c, g = None, [None] * 10
    for stretch in stretches:
        p = poles(stretch, scale)
        q = 1.0 - p
        if c is None:
            d = [jnp.ones_like(p), q]
            d.append(q * d[1])
            d.append(q * d[2])
        else:
            d = [c[0]]
            for k in range(1, 4):
                d.append(c[k] + q * d[k - 1])
        c = [p * x for x in d]
        if reflecting:
            e = [q * x for x in c]
            for n, (a, b) in enumerate(PAIRS):
                term = d[a] * e[b]
                g[n] = term if g[n] is None else g[n] + term
    return (c, g) if reflecting else c


def columns(tile):
    return [tile[:, i:i + 1] for i in range(B)]


def sweep(source, pole, mid, rows_of, first, second, sink=None):
    state = first
    for i in range(B):
        rows = pl.ds(i * B, B)
        p = pole[rows, :]
        state, w = cascade(state, source[rows_of(i), :], p, 1.0 - p)
        mid[rows, :] = w
    ahead, state = state, second
    for i in reversed(range(B)):
        rows = pl.ds(i * B, B)
        p = pole[rows, :]
        state, w = cascade(state, mid[rows, :], p, 1.0 - p)
        if sink is not None:
            sink(i, w)
    return ahead + state


def chain(got, coefs, reply):
    zero = [jnp.zeros((1, W), jnp.float32)] * 4

    def at(ref, j, k):
        return ref[j, k:k + 1, :]

    s, entered = zero, []
    for j in range(NY):
        entered.append(s)
        for k in range(4):
            reply[j, k:k + 1, :] = s[k]
        s = toeplitz([at(coefs, j, k) for k in range(4)], s, [at(got, j, k) for k in range(4)])
    b = zero
    for j in reversed(range(NY)):
        for k in range(4):
            reply[j, 4 + k:5 + k, :] = b[k]
        g = [at(coefs, j, 4 + n) for n in range(10)]
        add = reflect(g, entered[j], [at(got, j, 4 + k) for k in range(4)])
        b = toeplitz([at(coefs, j, k) for k in range(4)], b, add)


def kernel(inc_hbm, vert_hbm, reach_hbm, sx_hbm, sy_hbm, out,
           inc, vert, reach_line, sx, sy, load_sem, u, px, py, mid,
           ends_x, pair, own, chips, passing, to_z, from_z, back, entering, ys1, yr1, ys2, yr2,
           tgy, sxs, sxr, sys_, syr, sent, z_sent, y_sent, beside_recv, chip_recv, lines_recv, pair_recv,
           z_recv, back_recv, gather_recv, reply_recv):
    gx, gy = lax.axis_index("gx"), lax.axis_index("gy")
    z, core = gx // 2, lax.rem(gx, 2)
    other = (gx + 1 - 2 * core, gy)
    owner = 2 * z + 1

    def peer_y(dy, dx):
        return lax.rem(gy // 4 + dy, 4) * 4 + lax.rem(gy + dx, 4)

    barrier = pltpu.get_barrier_semaphore()
    for offset in OFFSETS_Y:
        pl.semaphore_signal(barrier, inc=1, device_id=(owner, peer_y(*offset)), device_id_type=MESH)

    @pl.when(core == 1)
    def _():
        for offset in OFFSETS_Y:
            pl.semaphore_signal(barrier, inc=1, device_id=(owner - 1, peer_y(*offset)), device_id_type=MESH)

    for r in range(1, NX):
        pl.semaphore_signal(barrier, inc=1, device_id=(lax.rem(gx + r, NX), gy), device_id_type=MESH)

    loads = [pltpu.make_async_copy(src, dst, load_sem.at[n]) for n, (src, dst) in enumerate(
        [(sx_hbm, sx), (reach_hbm, reach_line), (vert_hbm, vert), (inc_hbm, inc), (sy_hbm, sy)])]
    for load in loads:
        load.start()

    def remote(src, dst, sent, got, device):
        return pltpu.make_async_remote_copy(src, dst, sent, got, device_id=device, device_id_type=MESH)

    def to_owners(src, dst, got):
        for offset in OFFSETS_Y:
            peer = peer_y(*offset)
            remote(src.at[peer], dst.at[core, gy], y_sent.at[0], got, (owner, peer)).start()

        @pl.when(core == 0)
        def _():
            remote(src.at[gy], dst.at[0, gy], y_sent.at[0], got, (owner, gy)).start()

        @pl.when(core == 1)
        def _():
            dst[1, gy] = src[gy]

    def wait_for(part, sem):
        pltpu.make_async_copy(part, part, sem).wait()

    def lanes(ct):
        return slice(ct * W, (ct + 1) * W)

    loads[0].wait()
    loads[1].wait()
    reach = reach_line[...].reshape(1, C)
    stretch_x = sx[...].T
    scale_x = reach * float(NX * B)
    scale_y = reach * float(NY * B)
    for i in range(B):
        for ct in range(CT):
            px[ct, pl.ds(i * B, B), :] = poles(stretch_x[:, i:i + 1], scale_x[:, lanes(ct)])
    loads[4].wait()
    stretch_y = sy[...]
    for half in range(2):
        sxs[half, :, 0:B] = stretch_x[8 * half:8 * half + 8]
        sys_.reshape(NY * 8, W)[pl.ds(64 * half, 8, stride=8), 0:B] = stretch_y[8 * half:8 * half + 8]
    loads[2].wait()
    loads[3].wait()
    mixed = jnp.dot(inc[...], vert[...], preferred_element_type=jnp.float32)
    for ct in range(CT):
        u[ct] = mixed[:, lanes(ct)]

    zeros = [jnp.zeros((B, W), jnp.float32)] * 4
    nothing = [jnp.zeros((8, W), jnp.float32)] * 4

    def along(i):
        return pl.ds(i * B, B)

    def across(i):
        return pl.ds(i, B, stride=B)

    for ct in range(CT):
        ends = sweep(u.at[ct], px.at[ct], mid.at[ct], along, zeros, zeros)
        for half in range(2):
            for k in range(8):
                ends_x[ct, half, k] = ends[k][8 * half:8 * half + 8]

    pl.semaphore_wait(barrier, NX + NY - 2 + core * (NY - 1))
    remote(sxs.at[1 - core], sxr.at[gx], sent.at[0], beside_recv.at[0], other).start()
    for r in (2, 1, 3):
        for c in range(2):
            peer = 2 * lax.rem(z + r, NZ) + c
            remote(sxs.at[c], sxr.at[gx], sent.at[0], chip_recv.at[z], (peer, gy)).start()
    for ct in range(CT):
        remote(ends_x.at[ct, 1 - core], pair.at[ct, core], sent.at[0], pair_recv.at[0], other).start()
    sxr[gx] = sxs[core]
    for ct in range(CT):
        pair[ct, core] = ends_x[ct, core]

    def start_z(ct, r, kind):
        peer = lax.rem(z + r, NZ)
        return remote(to_z.at[ct, kind], from_z.at[ct, z, kind], z_sent.at[0], z_recv.at[ct],
                      (2 * peer + core, gy))

    def blocks(ct):
        t0, t1 = [[own[ct, b, k] for k in range(4)] for b in range(2)]
        g1 = [own[ct, 1, 4 + n] for n in range(10)]
        return t0, t1, g1, [[pair[ct, b, k] for k in range(8)] for b in range(2)]

    def block_transfer(ct, b):
        t, g = transfer(columns(sxr[2 * z + b]), scale_x[:, lanes(ct)], True)
        for k, value in enumerate(t + g):
            own[ct, b, k] = value

    for ct in range(CT):
        block_transfer(ct, core)
    wait_for(sxr.at[0], beside_recv.at[0])
    for ct in range(CT):
        block_transfer(ct, 1 - core)
        if ct == 0:
            wait_for(chips.reshape(NZ * CT * 14, 8, W).at[pl.ds(0, 8 * CT)], pair_recv.at[0])
        t0, t1, g1, (e0, e1) = blocks(ct)
        ahead = toeplitz(t1, e0[:4], e1[:4])
        behind = toeplitz(t0, reflect(g1, e0[:4], e1[4:]), e0[4:])
        for k in range(4):
            to_z[ct, 0, k] = ahead[k]
            to_z[ct, 1, k] = behind[k]
        for r in (2, 1, 3):
            pl.when(z < NZ - 1)(lambda ct=ct, r=r: start_z(ct, r, 0).start())
            pl.when(lax.rem(z + r, NZ) < z)(lambda ct=ct, r=r: start_z(ct, r, 1).start())

    to_owners(sys_, syr, lines_recv.at[0])

    def stretches(m):
        wait_for(sxr.at[pl.ds(0, 2)], chip_recv.at[m])
        return columns(sxr[2 * m]) + columns(sxr[2 * m + 1])

    def left(m, _):
        rates = stretches(m)
        for ct in range(CT):
            for k, value in enumerate(transfer(rates, scale_x[:, lanes(ct)], False)):
                chips[m, ct, k] = value
        return 0

    def right(m, _):
        rates = stretches(m)
        for ct in range(CT):
            t, g = transfer(rates, scale_x[:, lanes(ct)], True)
            for k, value in enumerate(t + g):
                chips[m, ct, k] = value
        return 0

    lax.fori_loop(0, z, left, 0)
    lax.fori_loop(z + 1, NZ, right, 0)
    for i in range(B):
        for ct in range(CT):
            py[ct, pl.ds(i * B, B), :] = poles(stretch_y[:, i:i + 1], scale_y[:, lanes(ct)])

    for ct in range(CT):
        for chip_z, messages in enumerate((5, 4, 3, 3)):
            pl.when(z == chip_z)(lambda ct=ct, messages=messages: wait_for(
                from_z.at[ct].reshape(2 * NZ, 4, 8, W).at[pl.ds(0, messages)], z_recv.at[ct]))

        def chip(m):
            return [chips[m, ct, k] for k in range(4)]

        def came(m, kind):
            return [from_z[ct, m, kind, k] for k in range(4)]

        def ahead(m, s):
            return toeplitz(chip(m), s, came(m, 0))

        def onward(m, s):
            s = ahead(m, s)
            for k in range(4):
                passing[ct, m + 1, k] = s[k]
            return s

        def behind(i, b):
            m = NZ - 1 - i
            g = [chips[m, ct, 4 + n] for n in range(10)]
            return toeplitz(chip(m), b, reflect(g, [passing[ct, m, k] for k in range(4)], came(m, 1)))

        s0 = lax.fori_loop(0, z, ahead, nothing)
        t0, t1, g1, (e0, e1) = blocks(ct)
        s1 = toeplitz(t0, s0, e0[:4])
        s2 = toeplitz(t1, s1, e1[:4])
        for k in range(4):
            passing[ct, z + 1, k] = s2[k]
        lax.fori_loop(z + 1, NZ - 1, onward, s2)
        b1 = lax.fori_loop(0, NZ - 1 - z, behind, nothing)
        b0 = toeplitz(t1, b1, reflect(g1, s1, e1[4:]))
        for b, states in enumerate([s0 + b0, s1 + b1]):
            for k in range(8):
                back[ct, b, k] = states[k]
        remote(back.at[ct, 1 - core], entering.at[ct, core], sent.at[0], back_recv.at[ct], other).start()
        entering[ct, core] = back[ct, core]


    for ct in range(CT):
        wait_for(entering.at[ct, 0], back_recv.at[ct])
        states = [jnp.concatenate([entering[ct, half, k] for half in range(2)], axis=0) for k in range(8)]

        def keep(i, w):
            u[ct, along(i), :] = w

        sweep(u.at[ct], px.at[ct], mid.at[ct], along, states[:4], states[4:], keep)
        ends = sweep(u.at[ct], py.at[ct], mid.at[ct], across, zeros, zeros)
        flat = ys1.at[ct].reshape(NY * 8, W)
        for k in range(8):
            for l in range(2):
                flat[pl.ds(64 * l + k, 8, stride=8), :] = ends[k][8 * l:8 * l + 8]
        to_owners(ys1.at[ct], yr1.at[ct], gather_recv.at[ct, core])

    @pl.when(core == 1)
    def _():
        wait_for(syr.reshape(2 * NY, 8, W).at[pl.ds(0, 2 * NY - 1)], lines_recv.at[0])
        for b in (1, 0):
            rates = columns(syr.at[b].reshape(NY * 8, W)[pl.ds(0, NY, stride=8), 0:B])
            for ct in range(CT):
                t, g = transfer(rates, scale_y[:, lanes(ct)], True)
                flat = tgy.at[b, ct].reshape(NY * 16, W)
                for k, value in enumerate(t + g):
                    for l in range(2):
                        flat[pl.ds(128 * l + k, 8, stride=16), :] = value[8 * l:8 * l + 8]
        for b, ct in ORDER:
            wait_for(yr1.at[ct, b, pl.ds(0, NY - b)], gather_recv.at[ct, b])
            chain(yr1.at[ct, b], tgy.at[b, ct], ys2.at[ct, b])
            for offset in OFFSETS_Y:
                peer = peer_y(*offset)
                remote(ys2.at[ct, b, peer], yr2.at[ct, gy], y_sent.at[0], reply_recv.at[ct],
                       (owner - 1 + b, peer)).start()
            if b == 0:
                remote(ys2.at[ct, 0, gy], yr2.at[ct, gy], y_sent.at[0], reply_recv.at[ct], (owner - 1, gy)).start()
            else:
                yr2[ct, gy] = ys2[ct, 1, gy]

    amplitude = 10.0 * jnp.minimum(reach, 0.25) * math.sqrt(NX * B * NY * B)
    for ct in range(CT):
        for b in range(2):
            pl.when(core == b)(lambda ct=ct, b=b: wait_for(yr2.at[ct, pl.ds(0, NY - b)], reply_recv.at[ct]))
        flat = yr2.at[ct].reshape(NY * 8, W)
        states = [flat[pl.ds(k, NY, stride=8), :] for k in range(8)]

        def finish(i, w):
            u[ct, across(i), :] = w * amplitude[:, lanes(ct)]

        sweep(u.at[ct], py.at[ct], mid.at[ct], across, states[:4], states[4:], finish)
        out[:, lanes(ct)] = u[ct]

    tiles = chips.reshape(NZ * CT * 14, 8, W)
    wait_for(tiles.at[pl.ds(0, NX - 1 + 16 * CT)], sent.at[0])
    for chip_z, messages in enumerate((3, 4, 5, 3)):
        pl.when(z == chip_z)(lambda messages=messages: wait_for(tiles.at[pl.ds(0, 4 * CT * messages)], z_sent.at[0]))
    for b, messages in enumerate(((CT + 1) * NY, (CT + 1) * (NY - 1) + CT * (2 * NY - 1))):
        pl.when(core == b)(lambda messages=messages: wait_for(tiles.at[pl.ds(0, messages)], y_sent.at[0]))


def shards(increment, vertical, col_reach, stretch_x, stretch_y):
    f32 = jnp.float32
    field = pltpu.VMEM((CT, B * B, W), f32)

    def states(*lead):
        return pltpu.VMEM(lead + (8, W), f32)

    def dma(*shape):
        return pltpu.SemaphoreType.DMA(shape)

    two, lines, both = states(CT, 2, 8), states(CT, NY), states(CT, 2, NY)
    operands = (increment.reshape(B * B, C), vertical, col_reach, stretch_x, stretch_y)
    result = pl.pallas_call(
        kernel,
        out_shape=jax.ShapeDtypeStruct((B * B, C), f32),
        in_specs=[pl.BlockSpec(memory_space=pltpu.HBM)] * 5,
        out_specs=pl.BlockSpec(memory_space=pltpu.VMEM),
        scratch_shapes=[
            pltpu.VMEM((B * B, C), jnp.bfloat16), pltpu.VMEM((C, C), jnp.bfloat16), pltpu.VMEM((C,), f32),
            pltpu.VMEM((B, B), f32), pltpu.VMEM((B, B), f32), dma(5),
            field, field, field, field,
            two, two, states(CT, 2, 14), states(NZ, CT, 14), states(CT, NZ + 1, 4),
            states(CT, 2, 4), states(CT, NZ, 2, 4), two, two,
            lines, both, both, lines, pltpu.VMEM((2, CT, NY, 16, W), f32),
            states(2), states(NX), states(NY), states(2, NY),
            dma(1), dma(1), dma(1), dma(1), dma(NZ), dma(1), dma(1),
            dma(CT), dma(CT), dma(CT, 2), dma(CT),
        ],
        compiler_params=pltpu.CompilerParams(
            collective_id=0, has_side_effects=True, vmem_limit_bytes=32 * 2**20),
        name="covariance",
    )(*[pltpu.with_memory_space_constraint(x, pltpu.HBM) for x in operands])
    return result.reshape(B, B, C)


def solution(mesh):
    in_specs = (P("gx", "gy", None), P(), P(), P("gx", "gy"), P("gx", "gy"))
    out_specs = P("gx", "gy", None)
    return jax.shard_map(shards, mesh=mesh, in_specs=in_specs, out_specs=out_specs, check_vma=False)
```

```python
import functools
import math

import jax
import jax.numpy as jnp
from jax import lax
from jax.experimental import pallas as pl
from jax.experimental.pallas import tpu as pltpu
from jax.sharding import PartitionSpec as P

MESH = pl.DeviceIdType.MESH
B = 16
NX, NY, NZ = 8, 16, 4
C, W, CT = 384, 128, 3
OFFSETS_Y = sorted([(a, b) for a in range(4) for b in range(4) if a or b],
                   key=lambda o: -min(o[0], 4 - o[0]) - min(o[1], 4 - o[1]))
ORDER = ((1, 0), (1, 1), (0, 0), (1, 2), (0, 1), (0, 2))
PAIRS = [(a, b) for a in range(4) for b in range(a, 4)]


def cascade(state, u, p, q):
    out = []
    for k in range(4):
        u = p * state[k] + q * u
        out.append(u)
    return out, u


def toeplitz(t, s, add):
    out = []
    for k in range(4):
        total = add[k]
        for m in range(k + 1):
            total = total + t[k - m] * s[m]
        out.append(total)
    return out


def reflect(g, s, add):
    out = []
    for a in range(4):
        total = add[a]
        for m in range(4):
            total = total + g[PAIRS.index((min(a, 3 - m), max(a, 3 - m)))] * s[m]
        out.append(total)
    return out


def poles(stretch, scale):
    return jnp.exp(-1.0 / (stretch * scale))


def transfer(stretches, scale, reflecting):
    c, g = None, [None] * 10
    for stretch in stretches:
        p = poles(stretch, scale)
        q = 1.0 - p
        if c is None:
            d = [jnp.ones_like(p), q]
            d.append(q * d[1])
            d.append(q * d[2])
        else:
            d = [c[0]]
            for k in range(1, 4):
                d.append(c[k] + q * d[k - 1])
        c = [p * x for x in d]
        if reflecting:
            e = [q * x for x in c]
            for n, (a, b) in enumerate(PAIRS):
                term = d[a] * e[b]
                g[n] = term if g[n] is None else g[n] + term
    return (c, g) if reflecting else c


def columns(tile):
    return [tile[:, i:i + 1] for i in range(B)]


def sweep(source, pole, mid, rows_of, first, second, sink=None):
    state = first
    for i in range(B):
        rows = pl.ds(i * B, B)
        p = pole[rows, :]
        state, w = cascade(state, source[rows_of(i), :], p, 1.0 - p)
        mid[rows, :] = w
    ahead, state = state, second
    for i in reversed(range(B)):
        rows = pl.ds(i * B, B)
        p = pole[rows, :]
        state, w = cascade(state, mid[rows, :], p, 1.0 - p)
        if sink is not None:
            sink(i, w)
    return ahead + state


def chain(got, coefs, reply):
    zero = [jnp.zeros((1, W), jnp.float32)] * 4

    def at(ref, j, k):
        return ref[j, k:k + 1, :]

    s, entered = zero, []
    for j in range(NY):
        entered.append(s)
        for k in range(4):
            reply[j, k:k + 1, :] = s[k]
        s = toeplitz([at(coefs, j, k) for k in range(4)], s, [at(got, j, k) for k in range(4)])
    b = zero
    for j in reversed(range(NY)):
        for k in range(4):
            reply[j, 4 + k:5 + k, :] = b[k]
        g = [at(coefs, j, 4 + n) for n in range(10)]
        add = reflect(g, entered[j], [at(got, j, 4 + k) for k in range(4)])
        b = toeplitz([at(coefs, j, k) for k in range(4)], b, add)


def kernel(inc_hbm, vert_hbm, reach_hbm, sx_hbm, sy_hbm, out,
           inc, vert, reach_line, sx, sy, load_sem, u, px, py, mid,
           ends_x, pair, own, chips, passing, to_z, from_z, back, entering, ys1, yr1, ys2, yr2,
           tgy, sxs, sxr, sys_, syr, sent, z_sent, y_sent, beside_recv, chip_recv, lines_recv, pair_recv,
           z_recv, back_recv, gather_recv, reply_recv):
    gx, gy = lax.axis_index("gx"), lax.axis_index("gy")
    z, core = gx // 2, lax.rem(gx, 2)
    other = (gx + 1 - 2 * core, gy)
    owner = 2 * z + 1

    def peer_y(dy, dx):
        return lax.rem(gy // 4 + dy, 4) * 4 + lax.rem(gy + dx, 4)

    barrier = pltpu.get_barrier_semaphore()
    for offset in OFFSETS_Y:
        pl.semaphore_signal(barrier, inc=1, device_id=(owner, peer_y(*offset)), device_id_type=MESH)

    @pl.when(core == 1)
    def _():
        for offset in OFFSETS_Y:
            pl.semaphore_signal(barrier, inc=1, device_id=(owner - 1, peer_y(*offset)), device_id_type=MESH)

    for r in range(1, NX):
        pl.semaphore_signal(barrier, inc=1, device_id=(lax.rem(gx + r, NX), gy), device_id_type=MESH)

    loads = [pltpu.make_async_copy(src, dst, load_sem.at[n]) for n, (src, dst) in enumerate(
        [(sx_hbm, sx), (reach_hbm, reach_line), (vert_hbm, vert), (inc_hbm, inc), (sy_hbm, sy)])]
    for load in loads:
        load.start()

    def remote(src, dst, sent, got, device):
        return pltpu.make_async_remote_copy(src, dst, sent, got, device_id=device, device_id_type=MESH)

    def to_owners(src, dst, got):
        for offset in OFFSETS_Y:
            peer = peer_y(*offset)
            remote(src.at[peer], dst.at[core, gy], y_sent.at[0], got, (owner, peer)).start()

        @pl.when(core == 0)
        def _():
            remote(src.at[gy], dst.at[0, gy], y_sent.at[0], got, (owner, gy)).start()

        @pl.when(core == 1)
        def _():
            dst[1, gy] = src[gy]

    def wait_for(part, sem):
        pltpu.make_async_copy(part, part, sem).wait()

    def lanes(ct):
        return slice(ct * W, (ct + 1) * W)

    loads[0].wait()
    loads[1].wait()
    reach = reach_line[...].reshape(1, C)
    stretch_x = sx[...].T
    scale_x = reach * float(NX * B)
    scale_y = reach * float(NY * B)
    for i in range(B):
        for ct in range(CT):
            px[ct, pl.ds(i * B, B), :] = poles(stretch_x[:, i:i + 1], scale_x[:, lanes(ct)])
    loads[4].wait()
    stretch_y = sy[...]
    for half in range(2):
        sxs[half, :, 0:B] = stretch_x[8 * half:8 * half + 8]
        sys_.reshape(NY * 8, W)[pl.ds(64 * half, 8, stride=8), 0:B] = stretch_y[8 * half:8 * half + 8]
    loads[2].wait()
    loads[3].wait()
    mixed = jnp.dot(inc[...], vert[...], preferred_element_type=jnp.float32)
    for ct in range(CT):
        u[ct] = mixed[:, lanes(ct)]

    zeros = [jnp.zeros((B, W), jnp.float32)] * 4
    nothing = [jnp.zeros((8, W), jnp.float32)] * 4

    def along(i):
        return pl.ds(i * B, B)

    def across(i):
        return pl.ds(i, B, stride=B)

    for ct in range(CT):
        ends = sweep(u.at[ct], px.at[ct], mid.at[ct], along, zeros, zeros)
        for half in range(2):
            for k in range(8):
                ends_x[ct, half, k] = ends[k][8 * half:8 * half + 8]

    pl.semaphore_wait(barrier, NX + NY - 2 + core * (NY - 1))
    remote(sxs.at[1 - core], sxr.at[gx], sent.at[0], beside_recv.at[0], other).start()
    for r in (2, 1, 3):
        for c in range(2):
            peer = 2 * lax.rem(z + r, NZ) + c
            remote(sxs.at[c], sxr.at[gx], sent.at[0], chip_recv.at[z], (peer, gy)).start()
    for ct in range(CT):
        remote(ends_x.at[ct, 1 - core], pair.at[ct, core], sent.at[0], pair_recv.at[0], other).start()
    sxr[gx] = sxs[core]
    for ct in range(CT):
        pair[ct, core] = ends_x[ct, core]

    def start_z(ct, r, kind):
        peer = lax.rem(z + r, NZ)
        return remote(to_z.at[ct, kind], from_z.at[ct, z, kind], z_sent.at[0], z_recv.at[ct],
                      (2 * peer + core, gy))

    def blocks(ct):
        t0, t1 = [[own[ct, b, k] for k in range(4)] for b in range(2)]
        g1 = [own[ct, 1, 4 + n] for n in range(10)]
        return t0, t1, g1, [[pair[ct, b, k] for k in range(8)] for b in range(2)]

    def block_transfer(ct, b):
        t, g = transfer(columns(sxr[2 * z + b]), scale_x[:, lanes(ct)], True)
        for k, value in enumerate(t + g):
            own[ct, b, k] = value

    for ct in range(CT):
        block_transfer(ct, core)
    wait_for(sxr.at[0], beside_recv.at[0])
    for ct in range(CT):
        block_transfer(ct, 1 - core)
        if ct == 0:
            wait_for(chips.reshape(NZ * CT * 14, 8, W).at[pl.ds(0, 8 * CT)], pair_recv.at[0])
        t0, t1, g1, (e0, e1) = blocks(ct)
        ahead = toeplitz(t1, e0[:4], e1[:4])
        behind = toeplitz(t0, reflect(g1, e0[:4], e1[4:]), e0[4:])
        for k in range(4):
            to_z[ct, 0, k] = ahead[k]
            to_z[ct, 1, k] = behind[k]
        for r in (2, 1, 3):
            pl.when(z < NZ - 1)(lambda ct=ct, r=r: start_z(ct, r, 0).start())
            pl.when(lax.rem(z + r, NZ) < z)(lambda ct=ct, r=r: start_z(ct, r, 1).start())

    to_owners(sys_, syr, lines_recv.at[0])

    def stretches(m):
        wait_for(sxr.at[pl.ds(0, 2)], chip_recv.at[m])
        return columns(sxr[2 * m]) + columns(sxr[2 * m + 1])

    def left(m, _):
        rates = stretches(m)
        for ct in range(CT):
            for k, value in enumerate(transfer(rates, scale_x[:, lanes(ct)], False)):
                chips[m, ct, k] = value
        return 0

    def right(m, _):
        rates = stretches(m)
        for ct in range(CT):
            t, g = transfer(rates, scale_x[:, lanes(ct)], True)
            for k, value in enumerate(t + g):
                chips[m, ct, k] = value
        return 0

    lax.fori_loop(0, z, left, 0)
    lax.fori_loop(z + 1, NZ, right, 0)
    for i in range(B):
        for ct in range(CT):
            py[ct, pl.ds(i * B, B), :] = poles(stretch_y[:, i:i + 1], scale_y[:, lanes(ct)])

    def leave_z(ct):
        for chip_z, messages in enumerate((5, 4, 3, 3)):
            pl.when(z == chip_z)(lambda ct=ct, messages=messages: wait_for(
                from_z.at[ct].reshape(2 * NZ, 4, 8, W).at[pl.ds(0, messages)], z_recv.at[ct]))

        def chip(m):
            return [chips[m, ct, k] for k in range(4)]

        def came(m, kind):
            return [from_z[ct, m, kind, k] for k in range(4)]

        def ahead(m, s):
            return toeplitz(chip(m), s, came(m, 0))

        def onward(m, s):
            s = ahead(m, s)
            for k in range(4):
                passing[ct, m + 1, k] = s[k]
            return s

        def behind(i, b):
            m = NZ - 1 - i
            g = [chips[m, ct, 4 + n] for n in range(10)]
            return toeplitz(chip(m), b, reflect(g, [passing[ct, m, k] for k in range(4)], came(m, 1)))

        s0 = lax.fori_loop(0, z, ahead, nothing)
        t0, t1, g1, (e0, e1) = blocks(ct)
        s1 = toeplitz(t0, s0, e0[:4])
        s2 = toeplitz(t1, s1, e1[:4])
        for k in range(4):
            passing[ct, z + 1, k] = s2[k]
        lax.fori_loop(z + 1, NZ - 1, onward, s2)
        b1 = lax.fori_loop(0, NZ - 1 - z, behind, nothing)
        b0 = toeplitz(t1, b1, reflect(g1, s1, e1[4:]))
        for b, states in enumerate([s0 + b0, s1 + b1]):
            for k in range(8):
                back[ct, b, k] = states[k]
        remote(back.at[ct, 1 - core], entering.at[ct, core], sent.at[0], back_recv.at[ct], other).start()
        entering[ct, core] = back[ct, core]


    def enter_y(ct):
        wait_for(entering.at[ct, 0], back_recv.at[ct])
        states = [jnp.concatenate([entering[ct, half, k] for half in range(2)], axis=0) for k in range(8)]

        def keep(i, w):
            u[ct, along(i), :] = w

        sweep(u.at[ct], px.at[ct], mid.at[ct], along, states[:4], states[4:], keep)
        ends = sweep(u.at[ct], py.at[ct], mid.at[ct], across, zeros, zeros)
        flat = ys1.at[ct].reshape(NY * 8, W)
        for k in range(8):
            for l in range(2):
                flat[pl.ds(64 * l + k, 8, stride=8), :] = ends[k][8 * l:8 * l + 8]
        to_owners(ys1.at[ct], yr1.at[ct], gather_recv.at[ct, core])

    for stage, ct in ((leave_z, 0), (leave_z, 1), (enter_y, 0), (leave_z, 2), (enter_y, 1), (enter_y, 2)):
        stage(ct)

    @pl.when(core == 1)
    def _():
        wait_for(syr.reshape(2 * NY, 8, W).at[pl.ds(0, 2 * NY - 1)], lines_recv.at[0])
        for b in (1, 0):
            rates = columns(syr.at[b].reshape(NY * 8, W)[pl.ds(0, NY, stride=8), 0:B])
            for ct in range(CT):
                t, g = transfer(rates, scale_y[:, lanes(ct)], True)
                flat = tgy.at[b, ct].reshape(NY * 16, W)
                for k, value in enumerate(t + g):
                    for l in range(2):
                        flat[pl.ds(128 * l + k, 8, stride=16), :] = value[8 * l:8 * l + 8]
        for b, ct in ORDER:
            wait_for(yr1.at[ct, b, pl.ds(0, NY - b)], gather_recv.at[ct, b])
            chain(yr1.at[ct, b], tgy.at[b, ct], ys2.at[ct, b])
            for offset in OFFSETS_Y:
                peer = peer_y(*offset)
                remote(ys2.at[ct, b, peer], yr2.at[ct, gy], y_sent.at[0], reply_recv.at[ct],
                       (owner - 1 + b, peer)).start()
            if b == 0:
                remote(ys2.at[ct, 0, gy], yr2.at[ct, gy], y_sent.at[0], reply_recv.at[ct], (owner - 1, gy)).start()
            else:
                yr2[ct, gy] = ys2[ct, 1, gy]

    amplitude = 10.0 * jnp.minimum(reach, 0.25) * math.sqrt(NX * B * NY * B)
    for ct in range(CT):
        for b in range(2):
            pl.when(core == b)(lambda ct=ct, b=b: wait_for(yr2.at[ct, pl.ds(0, NY - b)], reply_recv.at[ct]))
        flat = yr2.at[ct].reshape(NY * 8, W)
        states = [flat[pl.ds(k, NY, stride=8), :] for k in range(8)]

        def finish(i, w):
            u[ct, across(i), :] = w * amplitude[:, lanes(ct)]

        sweep(u.at[ct], py.at[ct], mid.at[ct], across, states[:4], states[4:], finish)
        out[:, lanes(ct)] = u[ct]

    tiles = chips.reshape(NZ * CT * 14, 8, W)
    wait_for(tiles.at[pl.ds(0, NX - 1 + 16 * CT)], sent.at[0])
    for chip_z, messages in enumerate((3, 4, 5, 3)):
        pl.when(z == chip_z)(lambda messages=messages: wait_for(tiles.at[pl.ds(0, 4 * CT * messages)], z_sent.at[0]))
    for b, messages in enumerate(((CT + 1) * NY, (CT + 1) * (NY - 1) + CT * (2 * NY - 1))):
        pl.when(core == b)(lambda messages=messages: wait_for(tiles.at[pl.ds(0, messages)], y_sent.at[0]))


def shards(increment, vertical, col_reach, stretch_x, stretch_y):
    f32 = jnp.float32
    field = pltpu.VMEM((CT, B * B, W), f32)

    def states(*lead):
        return pltpu.VMEM(lead + (8, W), f32)

    def dma(*shape):
        return pltpu.SemaphoreType.DMA(shape)

    two, lines, both = states(CT, 2, 8), states(CT, NY), states(CT, 2, NY)
    operands = (increment.reshape(B * B, C), vertical, col_reach, stretch_x, stretch_y)
    result = pl.pallas_call(
        kernel,
        out_shape=jax.ShapeDtypeStruct((B * B, C), f32),
        in_specs=[pl.BlockSpec(memory_space=pltpu.HBM)] * 5,
        out_specs=pl.BlockSpec(memory_space=pltpu.VMEM),
        scratch_shapes=[
            pltpu.VMEM((B * B, C), jnp.bfloat16), pltpu.VMEM((C, C), jnp.bfloat16), pltpu.VMEM((C,), f32),
            pltpu.VMEM((B, B), f32), pltpu.VMEM((B, B), f32), dma(5),
            field, field, field, field,
            two, two, states(CT, 2, 14), states(NZ, CT, 14), states(CT, NZ + 1, 4),
            states(CT, 2, 4), states(CT, NZ, 2, 4), two, two,
            lines, both, both, lines, pltpu.VMEM((2, CT, NY, 16, W), f32),
            states(2), states(NX), states(NY), states(2, NY),
            dma(1), dma(1), dma(1), dma(1), dma(NZ), dma(1), dma(1),
            dma(CT), dma(CT), dma(CT, 2), dma(CT),
        ],
        compiler_params=pltpu.CompilerParams(
            collective_id=0, has_side_effects=True, vmem_limit_bytes=32 * 2**20),
        name="covariance",
    )(*[pltpu.with_memory_space_constraint(x, pltpu.HBM) for x in operands])
    return result.reshape(B, B, C)


def solution(mesh):
    in_specs = (P("gx", "gy", None), P(), P(), P("gx", "gy"), P("gx", "gy"))
    out_specs = P("gx", "gy", None)
    return jax.shard_map(shards, mesh=mesh, in_specs=in_specs, out_specs=out_specs, check_vma=False)
```
